256 devices in a mesh: sect: 8 (over z_lo, y), tile: 32 (over z_hi, x, core).
Axes of the slice: x: 4, y: 4, z: 8 (z_hi: 4, z_lo: 2; z = z_hi * 2 + z_lo), core: 2. Of those that a mesh axis runs over, the one named last changes fastest.
Arguments:
- irrep_counts: int32 [2], replicated, may hold values from 64 to 128
- chol_left: bfloat16 [896, 256, 128], P('sect', 'tile'), may hold values from -0.15625 to 0.15625
- chol_right: bfloat16 [896, 128, 256], P(None, 'sect'), may hold values from -0.15625 to 0.15625
- lam: bfloat16 [512, 256, 256], P('sect', 'tile'), may hold values from -6 to 6
Outputs:
- ladder: bfloat16 [512, 128, 128], P('tile', None, 'sect')
The draws below stay inside these ranges and needn't reach their ends.
Inputs may be any that keep to these rules, and one draw needn't show every extreme that they name: Orbital p of irrep k is live when p < irrep_counts[k].
All inputs are finite; a program needn't handle non-finite values.
Results may differ from the reference program's by a relative error of at most 0.0049.
Values may be sent and summed in bfloat16 or wider, within the bound.
A program may use at most 64 MiB of HBM per device.

```python
import jax
import jax.numpy as jnp
from jax import lax

VIRR = 128
NAUX = 896
OCC_PAIRS = 512
V = 256


def steps_of(own_key, extent, split, least, top_value):
    factor_of = 1.0
    for position, blocks in split:
        heights = jax.random.uniform(jax.random.fold_in(jax.random.fold_in(own_key, 6), position), (blocks,), jnp.float32, least / len(split), top_value / len(split))
        factor_of = factor_of * jnp.repeat(jnp.exp(heights), extent[position] // blocks).reshape((-1,) + (1,) * (len(extent) - 1 - position))
    return factor_of


def scatter_about(key, extent, spread, reach, cuts=(), kind=jnp.bfloat16):
    result = jax.random.normal(key, extent, jnp.float32) * spread
    if len(cuts) > 0:
        result = steps_of(key, extent, cuts, -0.22, 0.18) * result
    return jnp.clip(result, min=-reach, max=reach).astype(kind)


def setup_inputs(seed: int = 0) -> dict:
    key_list = jax.random.split(jax.random.key(seed), 5)
    irrep_counts = jax.random.randint(key_list[0], (2,), VIRR // 2, VIRR + 1).astype(jnp.int32)
    chol_left = scatter_about(key_list[1], (NAUX, V, VIRR), (1.0 / (V * NAUX ** 0.5) ** 0.5), 0.15625, ((0, 8), (1, 32)))
    chol_right = scatter_about(key_list[2], (NAUX, VIRR, V), (1.0 / (V * NAUX ** 0.5) ** 0.5), 0.15625, ((1, 8),))
    lam = scatter_about(key_list[3], (OCC_PAIRS, V, V), 1.0, 6.0, ((0, 8), (1, 32)))
    return dict(irrep_counts=irrep_counts, chol_left=chol_left, chol_right=chol_right, lam=lam)


def live_masks(irrep_counts):
    positions = jnp.arange(VIRR, dtype=jnp.int32)
    first_live = positions < irrep_counts[0]
    second_live = positions < irrep_counts[1]
    window = jnp.concatenate([first_live, second_live])
    return first_live, second_live, window


def reference(irrep_counts, chol_left, chol_right, lam):
    first_live, second_live, window = live_masks(irrep_counts)
    left_factor = jnp.where(window[None, :, None] & first_live[None, None, :], chol_left.astype(jnp.float32), jnp.float32(0.0))
    left_factor = left_factor.reshape(NAUX, V * VIRR)
    right_factor = jnp.where(second_live[None, :, None] & window[None, None, :], chol_right.astype(jnp.float32), jnp.float32(0.0))
    lam_full = lam.astype(jnp.float32)

    def ladder_column(orbital):
        column = lax.dynamic_index_in_dim(right_factor, orbital, 1, keepdims=False)
        coulomb = lax.dot_general(left_factor, column, (((0,), (0,)), ((), ())), preferred_element_type=jnp.float32)
        coulomb = lax.optimization_barrier(coulomb.astype(jnp.bfloat16)).astype(jnp.float32)
        coulomb = coulomb.reshape(V, VIRR, V)
        return lax.dot_general(lam_full, coulomb, (((1, 2), (0, 2)), ((), ())), preferred_element_type=jnp.float32)

    stacked = lax.map(ladder_column, jnp.arange(VIRR, dtype=jnp.int32))
    return jnp.transpose(stacked, (1, 2, 0)).astype(jnp.bfloat16)
```

```python
import functools

import jax
import jax.numpy as jnp
from jax import lax
from jax.experimental import pallas as pl
from jax.experimental.pallas import tpu as pltpu
from jax.sharding import PartitionSpec as P

MESH = pl.DeviceIdType.MESH
BF, F32 = jnp.bfloat16, jnp.float32
YN, XN, ZN = 4, 4, 4
SECTS = 2 * YN
QB, CB, AN, DN = 112, 8, 128, 256
QN = QB * SECTS
BN = 16
GROUPS, ROWS = 2, 32
RC, NB = 2, 4
STAGES = 14
STEP = QN // STAGES
Z_FIRST = (1, 1, 0, 1, 1, 0, 1, 0, 1, 1, 0, 1, 1, 0, 1, 0)
FAR_PLUS = (1, 0, 1, 0, 0, 1, 0, 1, 1, 0, 1, 0, 0, 1, 0, 1)


def kernel(counts, left, lam, right, out,
           lbuf, ltr, mbuf, rstage, rmat, coul, p32, pbf, rpair,
           s32, sbf, xfar, xfwd, xdir, u32, ubf, zfar, zfwd, zdir,
           rsem, ag_send, ag_recv, pr_send, pr_recv, x_send, x_recv, z_send, z_recv):
    sect, tile = lax.axis_index("sect"), lax.axis_index("tile")
    zl, y = sect // YN, sect % YN
    zh, x, core = tile // (2 * XN), (tile // 2) % XN, tile % 2
    base, obase = zl * YN, (1 - zl) * YN
    yp, ym, yf = (y + 1) % YN, (y + YN - 1) % YN, (y + 2) % YN
    at_yp, at_ym, at_z = {"sect": base + yp}, {"sect": base + ym}, {"sect": obase + y}

    def tile_at(zz, xx, cc):
        return {"tile": (zz * XN + xx) * 2 + cc}

    xp, xm, xf = (x + 1) % XN, (x + XN - 1) % XN, (x + 2) % XN
    zp, zm, zf = (zh + 1) % ZN, (zh + ZN - 1) % ZN, (zh + 2) % ZN
    at_xp, at_xm = tile_at(zh, xp, core), tile_at(zh, xm, core)
    at_zp, at_zm = tile_at(zp, x, core), tile_at(zm, x, core)
    at_pair = tile_at(zh, x, 1 - core)

    barrier = pltpu.get_barrier_semaphore()
    friends = (at_yp, at_ym, at_z, at_xp, at_xm, at_zp, at_zm, at_pair)
    for friend in friends:
        pl.semaphore_signal(barrier, inc=1, device_id=friend, device_id_type=MESH)

    def stage_copy(k):
        rows = pl.ds(k * STEP, STEP)
        return pltpu.make_async_copy(right.at[rows], rstage.at[rows], rsem.at[k])

    for k in range(STAGES):
        stage_copy(k).start()

    n1, n2 = counts[0], counts[1]
    own = pltpu.einshape("qca->cqa", left[...])
    lane = lax.broadcasted_iota(jnp.int32, (QB, AN), 1)
    for c in range(CB):
        orbital = tile * CB + c
        room = jnp.where(orbital < AN, n1 - orbital, n2 + AN - orbital)
        limit = jnp.where(room > 0, n1, 0)
        kept = jnp.where(lane < limit, own[c].astype(F32), 0.0).astype(BF)
        lbuf[c, pl.ds(pl.multiple_of(sect * QB, 16), QB), :] = kept
    lane = lax.broadcasted_iota(jnp.int32, (ROWS, DN), 1)
    d_live = lane < jnp.where(lane < AN, n1, n2 + AN)
    for g in range(GROUPS):
        mine = jnp.concatenate([lam[16 * u + 8 * g : 16 * u + 8 * g + 8] for u in range(4)], axis=0)
        mine = pltpu.einshape("icd->cid", mine)
        for c in range(CB):
            kept = jnp.where(d_live, mine[c].astype(F32), 0.0).astype(BF)
            mbuf[g, pl.ds(pl.multiple_of(sect * ROWS, 16), ROWS), c * DN : (c + 1) * DN] = kept

    sent = []

    def go(copy):
        copy.start()
        sent.append(copy)

    def piece(p, src):
        if p < 8:
            return lbuf.at[p, pl.ds(pl.multiple_of(src * QB, 16), QB), :]
        g, part = divmod(p - 8, 4)
        return mbuf.at[g, pl.ds(pl.multiple_of(src * ROWS, 16), ROWS), pl.ds(part * 2 * DN, 2 * DN)]

    def pass_on(p, src, k, where):
        ref = piece(p, src)
        go(pltpu.make_async_remote_copy(ref, ref, ag_send.at[p, k], ag_recv.at[p, src], where, MESH))

    def arrived(p, src):
        ref = piece(p, src)
        pltpu.make_async_remote_copy(ref, ref, ag_send.at[p, 0], ag_recv.at[p, src], at_z, MESH).wait_recv()

    def ag_own(p):
        if Z_FIRST[p]:
            pass_on(p, sect, 0, at_z)
        pass_on(p, sect, 1, at_yp)
        pass_on(p, sect, 2, at_ym)
        if not Z_FIRST[p]:
            pass_on(p, sect, 0, at_z)

    def ag_near(p):
        if Z_FIRST[p]:
            arrived(p, obase + y)
            pass_on(p, obase + y, 4, at_yp)
            pass_on(p, obase + y, 5, at_ym)
        arrived(p, base + ym)
        if FAR_PLUS[p]:
            pass_on(p, base + ym, 3, at_yp)
        if not Z_FIRST[p]:
            pass_on(p, base + ym, 4, at_z)
        arrived(p, base + yp)
        if not FAR_PLUS[p]:
            pass_on(p, base + yp, 3, at_ym)
        if not Z_FIRST[p]:
            pass_on(p, base + yp, 5, at_z)

    def ag_far(p):
        if Z_FIRST[p]:
            arrived(p, obase + ym)
            if FAR_PLUS[p]:
                pass_on(p, obase + ym, 6, at_yp)
            arrived(p, obase + yp)
            if not FAR_PLUS[p]:
                pass_on(p, obase + yp, 6, at_ym)
        else:
            arrived(p, base + yf)
            pass_on(p, base + yf, 6, at_z)

    def ag_end(p):
        if Z_FIRST[p]:
            arrived(p, base + yf)
            arrived(p, obase + yf)
        else:
            for other in (y, ym, yp, yf):
                arrived(p, obase + other)

    def relay(first, last):
        def body(k, carry):
            stage_copy(k).wait()
            rows = pl.ds(pl.multiple_of(k * STEP, 16), STEP)
            rmat[:, rows, :] = pltpu.einshape("qbd->bqd", rstage[rows])
            return carry

        lax.fori_loop(first, last, body, 0)

    def turn(h):
        for c in range(4 * h, 4 * h + 4):
            ltr[c * AN : (c + 1) * AN, :] = lbuf[c].T

    def coulomb(h, first, last):
        def body(b, carry):
            block = jnp.dot(ltr[h * 4 * AN : (h + 1) * 4 * AN, :], rmat[b], preferred_element_type=F32).astype(BF)
            for k in range(4):
                c = 4 * h + k
                coul[b, :, c * DN : (c + 1) * DN] = block[k * AN : (k + 1) * AN]
            return carry

        lax.fori_loop(first, last, body, 0)

    def ladder(g, r):
        def body(j, carry):
            pair = coul[pl.ds(2 * (r * NB + j), 2)].reshape(2 * AN, CB * DN)
            block = lax.dot_general(mbuf[g], pair, (((1,), (1,)), ((), ())), preferred_element_type=F32)
            block = block.reshape(ZN, XN, 2, 8, 2 * AN)
            block = jnp.concatenate([block[..., :AN], block[..., AN:]], axis=3)
            for cc in range(2):
                for xx in range(XN):
                    p32[g, r, cc, xx, :, j] = block[:, xx, cc]
                    pbf[g, r, cc, xx, :, j] = block[:, xx, cc].astype(BF)
            return carry

        lax.fori_loop(0, NB, body, 0)

    def pair_copy(g, r):
        return pltpu.make_async_remote_copy(
            pbf.at[g, r, 1 - core], rpair.at[g, r], pr_send.at[g, r], pr_recv.at[g, r], at_pair, MESH)

    def ring_copies(g, r, bf, far, fwd, direct, sends, recvs, cp, cm, cf, to_p, to_m):
        half = bf.shape[3] // 2
        lo, hi = pl.ds(0, half), pl.ds(half, half)
        ends = (
            (bf.at[g, r, cf, lo], far.at[g, r, 0], to_p),
            (bf.at[g, r, cf, hi], far.at[g, r, 1], to_m),
            (bf.at[g, r, cp, hi], direct.at[g, r, 0, hi], to_p),
            (bf.at[g, r, cm, lo], direct.at[g, r, 1, lo], to_m),
            (fwd.at[g, r, 0], direct.at[g, r, 0, lo], to_p),
            (fwd.at[g, r, 1], direct.at[g, r, 1, hi], to_m),
        )

        def copy(k):
            src, dst, where = ends[k]
            return pltpu.make_async_remote_copy(src, dst, sends.at[g, r, k], recvs.at[g, r, k], where, MESH)

        return copy

    def x_copies(g, r):
        return ring_copies(g, r, sbf, xfar, xfwd, xdir, x_send, x_recv, xp, xm, xf, at_xp, at_xm)

    def z_copies(g, r):
        return ring_copies(g, r, ubf, zfar, zfwd, zdir, z_send, z_recv, zp, zm, zf, at_zp, at_zm)

    def ring_mid(g, r, copies, total, far, fwd, cp, cm):
        half = total.shape[3] // 2
        copies(0).wait_recv()
        fwd[g, r, 0] = (total[g, r, cp, :half] + far[g, r, 0].astype(F32)).astype(BF)
        go(copies(4))
        copies(1).wait_recv()
        fwd[g, r, 1] = (total[g, r, cm, half:] + far[g, r, 1].astype(F32)).astype(BF)
        go(copies(5))

    def ring_end(g, r, copies, total, direct, me):
        for k in range(2, 6):
            copies(k).wait_recv()
        return total[g, r, me] + direct[g, r, 0].astype(F32) + direct[g, r, 1].astype(F32)

    def red1(g, r):
        ladder(g, r)
        go(pair_copy(g, r))

    def red2(g, r):
        pair_copy(g, r).wait_recv()
        for xx in range(XN):
            total = p32[g, r, core, xx] + rpair[g, r, xx].astype(F32)
            s32[g, r, xx] = total
            sbf[g, r, xx] = total.astype(BF)
        copies = x_copies(g, r)
        for k in range(4):
            go(copies(k))

    def red3(g, r):
        ring_mid(g, r, x_copies(g, r), s32, xfar, xfwd, xp, xm)

    def red4(g, r):
        total = ring_end(g, r, x_copies(g, r), s32, xdir, x)
        u32[g, r] = total
        ubf[g, r] = total.astype(BF)
        copies = z_copies(g, r)
        for k in range(4):
            go(copies(k))

    def red5(g, r):
        ring_mid(g, r, z_copies(g, r), u32, zfar, zfwd, zp, zm)

    def red6(g, r):
        out[g, r] = ring_end(g, r, z_copies(g, r), u32, zdir, zh)

    pl.semaphore_wait(barrier, len(friends))

    for p in range(8):
        ag_own(p)
    relay(0, 2)
    ag_near(0), ag_near(1)
    relay(2, 4)
    ag_near(2), ag_near(3)
    relay(4, 6)
    ag_near(4), ag_near(5), ag_far(0), ag_far(1)
    relay(6, 8)
    ag_near(6), ag_near(7), ag_far(2), ag_far(3)
    for p in range(8, 12):
        ag_own(p)
    relay(8, 10)
    ag_far(4), ag_far(5)
    relay(10, 12)
    ag_far(6), ag_far(7)
    relay(12, 14)
    for p in range(0, 4):
        ag_end(p)
    turn(0)
    coulomb(0, 0, 8)
    ag_near(8), ag_near(9)
    coulomb(0, 8, 16)
    ag_near(10), ag_near(11)
    for p in range(12, 16):
        ag_own(p)
    for p in range(4, 8):
        ag_end(p)
    turn(1)
    ag_far(8), ag_far(9)
    coulomb(1, 0, 8)
    ag_far(10), ag_far(11), ag_near(12), ag_near(13)
    coulomb(1, 8, 16)
    ag_near(14), ag_near(15)
    for p in range(8, 12):
        ag_end(p)
    red1(0, 0)
    ag_far(12), ag_far(13)
    red1(0, 1)
    ag_far(14), ag_far(15)
    red2(0, 0), red2(0, 1), red3(0, 0), red3(0, 1), red4(0, 0)
    for p in range(12, 16):
        ag_end(p)
    red1(1, 0)
    red4(0, 1)
    red1(1, 1)
    red5(0, 0), red5(0, 1)
    red2(1, 0), red2(1, 1)
    red6(0, 0), red6(0, 1)
    red3(1, 0), red3(1, 1), red4(1, 0), red4(1, 1), red5(1, 0), red5(1, 1), red6(1, 0), red6(1, 1)
    for copy in sent:
        copy.wait_send()


def per_device(irrep_counts, chol_left, chol_right, lam):
    whole = (GROUPS, RC)
    spot = (16, AN)
    vmem = pltpu.VMEM
    dma = pltpu.SemaphoreType.DMA
    summed = pl.pallas_call(
        kernel,
        out_shape=jax.ShapeDtypeStruct(whole + (NB,) + spot, F32),
        in_specs=[
            pl.BlockSpec(memory_space=pltpu.SMEM),
            pl.BlockSpec(memory_space=vmem),
            pl.BlockSpec(memory_space=vmem),
            pl.BlockSpec(memory_space=pl.ANY),
        ],
        out_specs=pl.BlockSpec(memory_space=vmem),
        scratch_shapes=[
            vmem((CB, QN, AN), BF),
            vmem((CB * AN, QN), BF),
            vmem((GROUPS, ROWS * SECTS, CB * DN), BF),
            vmem((QN, BN, DN), BF),
            vmem((BN, QN, DN), BF),
            vmem((BN, AN, CB * DN), BF),
            vmem(whole + (2, XN, ZN, NB) + spot, F32),
            vmem(whole + (2, XN, ZN, NB) + spot, BF),
            vmem(whole + (XN, ZN, NB) + spot, BF),
            vmem(whole + (XN, ZN, NB) + spot, F32),
            vmem(whole + (XN, ZN, NB) + spot, BF),
            vmem(whole + (2, ZN // 2, NB) + spot, BF),
            vmem(whole + (2, ZN // 2, NB) + spot, BF),
            vmem(whole + (2, ZN, NB) + spot, BF),
            vmem(whole + (ZN, NB) + spot, F32),
            vmem(whole + (ZN, NB) + spot, BF),
            vmem(whole + (2, NB // 2) + spot, BF),
            vmem(whole + (2, NB // 2) + spot, BF),
            vmem(whole + (2, NB) + spot, BF),
            dma((STAGES,)),
            dma((16, 7)),
            dma((16, SECTS)),
            dma(whole),
            dma(whole),
            dma(whole + (6,)),
            dma(whole + (6,)),
            dma(whole + (6,)),
            dma(whole + (6,)),
        ],
        compiler_params=pltpu.CompilerParams(
            collective_id=0, has_side_effects=True, vmem_limit_bytes=56 << 20
        ),
        cost_estimate=pl.CostEstimate(flops=12_000_000_000, bytes_accessed=8_000_000, transcendentals=0),
    )(irrep_counts, chol_left, lam, chol_right)
    summed = summed.reshape(GROUPS, RC, NB, 2, 8, AN)
    summed = jnp.transpose(summed, (0, 4, 5, 1, 2, 3)).reshape(GROUPS * 8, AN, BN)
    orbital = lax.axis_index("sect") * BN + lax.broadcasted_iota(jnp.int32, summed.shape, 2)
    return jnp.where(orbital < irrep_counts[1], summed, 0.0).astype(BF)


def solution(mesh):
    return jax.shard_map(
        per_device,
        mesh=mesh,
        in_specs=(P(), P("sect", "tile", None), P(None, "sect", None), P("sect", "tile", None)),
        out_specs=P("tile", None, "sect"),
        check_vma=False,
    )
```

```python
import functools

import jax
import jax.numpy as jnp
from jax import lax
from jax.experimental import pallas as pl
from jax.experimental.pallas import tpu as pltpu
from jax.sharding import PartitionSpec as P

MESH = pl.DeviceIdType.MESH
BF, F32 = jnp.bfloat16, jnp.float32
YN, XN, ZN = 4, 4, 4
SECTS = 2 * YN
QB, CB, AN, DN = 112, 8, 128, 256
QN = QB * SECTS
BN = 16
GROUPS, ROWS = 2, 32
RC, NB = 2, 4
STAGES = 14
STEP = QN // STAGES
Z_FIRST = (1, 0, 1, 0, 1, 0, 0, 0, 1, 1, 1, 1, 0, 0, 1, 1)
FAR_PLUS = (0, 1, 1, 0, 1, 0, 1, 1, 0, 0, 1, 1, 1, 0, 1, 0)


def kernel(counts, left, lam, right, out,
           lbuf, ltr, mbuf, rstage, rmat, coul, p32, pbf, rpair,
           s32, sbf, xfar, xfwd, xdir, u32, ubf, zfar, zfwd, zdir,
           v32, acc, rsem, ag_send, ag_recv, pr_send, pr_recv, x_send, x_recv, z_send, z_recv):
    sect, tile = lax.axis_index("sect"), lax.axis_index("tile")
    zl, y = sect // YN, sect % YN
    zh, x, core = tile // (2 * XN), (tile // 2) % XN, tile % 2
    base, obase = zl * YN, (1 - zl) * YN
    yp, ym, yf = (y + 1) % YN, (y + YN - 1) % YN, (y + 2) % YN
    at_yp, at_ym, at_z = {"sect": base + yp}, {"sect": base + ym}, {"sect": obase + y}

    bm, bp, bf = base + ym, base + yp, base + yf
    oy, om, op, of = obase + y, obase + ym, obase + yp, obase + yf

    def tile_at(zz, xx, cc):
        return {"tile": (zz * XN + xx) * 2 + cc}

    xp, xm, xf = (x + 1) % XN, (x + XN - 1) % XN, (x + 2) % XN
    zp, zm, zf = (zh + 1) % ZN, (zh + ZN - 1) % ZN, (zh + 2) % ZN
    at_xp, at_xm = tile_at(zh, xp, core), tile_at(zh, xm, core)
    at_zp, at_zm = tile_at(zp, x, core), tile_at(zm, x, core)
    at_pair = tile_at(zh, x, 1 - core)

    barrier = pltpu.get_barrier_semaphore()
    friends = (at_yp, at_ym, at_z, at_xp, at_xm, at_zp, at_zm, at_pair)
    for friend in friends:
        pl.semaphore_signal(barrier, inc=1, device_id=friend, device_id_type=MESH)

    def stage_copy(k):
        rows = pl.ds(k * STEP, STEP)
        return pltpu.make_async_copy(right.at[rows], rstage.at[rows], rsem.at[k])

    for k in range(STAGES):
        stage_copy(k).start()

    n1, n2 = counts[0], counts[1]
    own = pltpu.einshape("qca->cqa", left[...])
    lane = lax.broadcasted_iota(jnp.int32, (QB, AN), 1)
    for c in range(CB):
        orbital = tile * CB + c
        room = jnp.where(orbital < AN, n1 - orbital, n2 + AN - orbital)
        limit = jnp.where(room > 0, n1, 0)
        kept = jnp.where(lane < limit, own[c].astype(F32), 0.0).astype(BF)
        lbuf[c, pl.ds(pl.multiple_of(sect * QB, 16), QB), :] = kept
    lane = lax.broadcasted_iota(jnp.int32, (ROWS, DN), 1)
    d_live = lane < jnp.where(lane < AN, n1, n2 + AN)
    for g in range(GROUPS):
        mine = jnp.concatenate([lam[16 * u + 8 * g : 16 * u + 8 * g + 8] for u in range(4)], axis=0)
        mine = pltpu.einshape("icd->cid", mine)
        for c in range(CB):
            kept = jnp.where(d_live, mine[c].astype(F32), 0.0).astype(BF)
            mbuf[g, pl.ds(pl.multiple_of(sect * ROWS, 16), ROWS), c * DN : (c + 1) * DN] = kept

    sent = []

    def go(make):
        make().start()
        sent.append(make)

    def piece(p, src):
        if p < 8:
            return lbuf.at[p, pl.ds(pl.multiple_of(src * QB, 16), QB), :]
        g, part = divmod(p - 8, 4)
        return mbuf.at[g, pl.ds(pl.multiple_of(src * ROWS, 16), ROWS), pl.ds(part * 2 * DN, 2 * DN)]

    def pass_on(p, src, k, where):
        def make():
            ref = piece(p, src)
            return pltpu.make_async_remote_copy(ref, ref, ag_send.at[p, k], ag_recv.at[p, src], where, MESH)

        go(make)

    def arrived(p, src):
        ref = piece(p, src)
        pltpu.make_async_remote_copy(ref, ref, ag_send.at[p, 0], ag_recv.at[p, src], at_z, MESH).wait_recv()

    def ag_own(p):
        if Z_FIRST[p]:
            pass_on(p, sect, 0, at_z)
        pass_on(p, sect, 1, at_yp)
        pass_on(p, sect, 2, at_ym)
        if not Z_FIRST[p]:
            pass_on(p, sect, 0, at_z)

    def ag_near(p):
        if Z_FIRST[p]:
            arrived(p, oy)
            pass_on(p, oy, 4, at_yp)
            pass_on(p, oy, 5, at_ym)
        arrived(p, bm)
        if FAR_PLUS[p]:
            pass_on(p, bm, 3, at_yp)
        if not Z_FIRST[p]:
            pass_on(p, bm, 4, at_z)
        arrived(p, bp)
        if not FAR_PLUS[p]:
            pass_on(p, bp, 3, at_ym)
        if not Z_FIRST[p]:
            pass_on(p, bp, 5, at_z)

    def ag_far(p):
        if Z_FIRST[p]:
            arrived(p, om)
            if FAR_PLUS[p]:
                pass_on(p, om, 6, at_yp)
            arrived(p, op)
            if not FAR_PLUS[p]:
                pass_on(p, op, 6, at_ym)
        else:
            arrived(p, bf)
            pass_on(p, bf, 6, at_z)

    def ag_end(p):
        if Z_FIRST[p]:
            arrived(p, bf)
            arrived(p, of)
        else:
            for src in (oy, om, op, of):
                arrived(p, src)

    def loop(count, body, events):
        def step(j, carry):
            body(j)
            for k, todo in events.items():
                pl.when(j == k)(functools.partial(run, todo))
            return carry

        lax.fori_loop(0, count, step, 0)

    def run(todo):
        for name, *where in todo:
            ACTIONS[name](*where)

    def relay(events):
        def body(k):
            stage_copy(k).wait()
            rows = pl.ds(pl.multiple_of(k * STEP, 16), STEP)
            rmat[:, rows, :] = pltpu.einshape("qbd->bqd", rstage[rows])

        loop(STAGES, body, events)

    def turn(h):
        for c in range(4 * h, 4 * h + 4):
            ltr[c * AN : (c + 1) * AN, :] = lbuf[c].T

    def coulomb(h, events):
        def body(j):
            for b in (2 * j, 2 * j + 1):
                block = jnp.dot(ltr[h * 4 * AN : (h + 1) * 4 * AN, :], rmat[b], preferred_element_type=F32).astype(BF)
                for k in range(4):
                    c = 4 * h + k
                    coul[b, :, c * DN : (c + 1) * DN] = block[k * AN : (k + 1) * AN]

        loop(BN // 2, body, events)

    def product(g, quad, first, last):
        cols = coul[pl.ds(4 * quad, 4), :, first * DN : last * DN].reshape(4 * AN, (last - first) * DN)
        rows = mbuf[g, :, first * DN : last * DN]
        return lax.dot_general(rows, cols, (((1,), (1,)), ((), ())), preferred_element_type=F32)

    def early(g, events):
        def body(quad):
            acc[quad] = product(g, quad, 0, CB // 2)

        loop(BN // 4, body, events)

    def ladder(g, r, events):
        def body(k):
            quad = r * (NB // 2) + k
            block = product(g, quad, 0, CB) if g == 0 else acc[quad] + product(g, quad, CB // 2, CB)
            for m in range(2):
                part = block[:, 2 * AN * m : 2 * AN * (m + 1)].reshape(ZN, XN, 2, 8, 2 * AN)
                part = jnp.concatenate([part[..., :AN], part[..., AN:]], axis=3)
                for cc in range(2):
                    for xx in range(XN):
                        p32[g, r, cc, xx, :, 2 * k + m] = part[:, xx, cc]
                        pbf[g, r, cc, xx, :, 2 * k + m] = part[:, xx, cc].astype(BF)

        loop(NB // 2, body, events)

    def pair_copy(g, r):
        return pltpu.make_async_remote_copy(
            pbf.at[g, r, 1 - core], rpair.at[g, r], pr_send.at[g, r], pr_recv.at[g, r], at_pair, MESH)

    def ring_copies(g, r, bf, far, fwd, direct, sends, recvs, cp, cm, cf, to_p, to_m):
        half = bf.shape[3] // 2
        lo, hi = pl.ds(0, half), pl.ds(half, half)
        ends = (
            (bf.at[g, r, cf, lo], far.at[g, r, 0], to_p),
            (bf.at[g, r, cf, hi], far.at[g, r, 1], to_m),
            (bf.at[g, r, cp, hi], direct.at[g, r, 0, hi], to_p),
            (bf.at[g, r, cm, lo], direct.at[g, r, 1, lo], to_m),
            (fwd.at[g, r, 0], direct.at[g, r, 0, lo], to_p),
            (fwd.at[g, r, 1], direct.at[g, r, 1, hi], to_m),
        )

        def copy(k):
            src, dst, where = ends[k]
            return pltpu.make_async_remote_copy(src, dst, sends.at[g, r, k], recvs.at[g, r, k], where, MESH)

        return copy

    def x_copies(g, r):
        return ring_copies(g, r, sbf, xfar, xfwd, xdir, x_send, x_recv, xp, xm, xf, at_xp, at_xm)

    def z_copies(g, r):
        return ring_copies(g, r, ubf, zfar, zfwd, zdir, z_send, z_recv, zp, zm, zf, at_zp, at_zm)

    def ring_mid(g, r, ring, total, far, fwd, cp, cm):
        half = total.shape[3] // 2
        copies = ring(g, r)
        copies(0).wait_recv()
        fwd[g, r, 0] = (total[g, r, cp, :half] + far[g, r, 0].astype(F32)).astype(BF)
        go(lambda: ring(g, r)(4))
        copies(1).wait_recv()
        fwd[g, r, 1] = (total[g, r, cm, half:] + far[g, r, 1].astype(F32)).astype(BF)
        go(lambda: ring(g, r)(5))

    def ring_end(g, r, copies, total, direct, me):
        for k in range(2, 6):
            copies(k).wait_recv()
        return total[g, r, me] + direct[g, r, 0].astype(F32) + direct[g, r, 1].astype(F32)

    def red1(g, r):
        go(functools.partial(pair_copy, g, r))

    def red2(g, r):
        pair_copy(g, r).wait_recv()
        for xx in range(XN):
            total = p32[g, r, core, xx] + rpair[g, r, xx].astype(F32)
            s32[g, r, xx] = total
            sbf[g, r, xx] = total.astype(BF)
        for k in range(4):
            go(functools.partial(lambda k: x_copies(g, r)(k), k))

    def red3(g, r):
        ring_mid(g, r, x_copies, s32, xfar, xfwd, xp, xm)

    def red4(g, r):
        total = ring_end(g, r, x_copies(g, r), s32, xdir, x)
        u32[g, r] = total
        ubf[g, r] = total.astype(BF)
        for k in range(4):
            go(functools.partial(lambda k: z_copies(g, r)(k), k))

    def red5(g, r):
        ring_mid(g, r, z_copies, u32, zfar, zfwd, zp, zm)

    def red6(g, r):
        v32[g, r * NB : (r + 1) * NB] = ring_end(g, r, z_copies(g, r), u32, zdir, zh)

    def finish(g):
        summed = pltpu.einshape("bia->iba", v32[g].reshape(BN, 8, AN))
        orbital = sect * BN + lax.broadcasted_iota(jnp.int32, summed.shape, 1)
        out[8 * g : 8 * g + 8] = jnp.where(orbital < n2, summed, 0.0).astype(BF)

    ACTIONS = dict(o=ag_own, n=ag_near, f=ag_far, e=ag_end, r1=red1, r2=red2, r3=red3, r4=red4, r5=red5, r6=red6, end=finish)

    pl.semaphore_wait(barrier, len(friends))

    def act(text):
        words = text.split()
        return [(w[:2], int(w[2]), int(w[3])) if w[0] == "r" else (w[0], int(w[1:])) for w in words]

    run(act("o0 o1 o2 o3 o4"))
    relay({7: act("o5 n0"), 9: act("n1"), 10: act("n2"), 12: act("n3")})
    run(act("n4 n5 f0 o6 f1 o7 f2 f3 o8 f4 o9 f5 o10 o11 n6 n7 o12 e0 e1 e2 e3"))
    turn(0)
    run(act("o13"))
    coulomb(0, {0: act("o14 n8 n9"), 2: act("n10 f6 n11 f7"), 3: act("n12"), 4: act("n13"), 5: act("o15 f8"), 6: act("f9 n14 f10")})
    run(act("e4 e5 e6 e7"))
    turn(1)
    run(act("f11 f13"))
    coulomb(1, {1: act("f12"), 2: act("f14"), 3: act("n15")})
    run(act("e8 e9 e10 e11"))
    ladder(0, 0, {0: act("f15")})
    run(act("r100"))
    ladder(0, 1, {})
    run(act("r101 r200 e12 e13"))
    early(1, {2: act("r201")})
    run(act("e14 e15"))
    ladder(1, 0, {})
    run(act("r110 r300"))
    ladder(1, 1, {})
    run(act("r111 r301 r210 r211 r400 r401 r310 r311 r500 r501 r410 r411 r600 r601 r510 r511 r610 r611"))
    finish(0)
    finish(1)
    for make in sent:
        make().wait_send()


def per_device(irrep_counts, chol_left, chol_right, lam):
    whole = (GROUPS, RC)
    spot = (16, AN)
    vmem = pltpu.VMEM
    dma = pltpu.SemaphoreType.DMA
    summed = pl.pallas_call(
        kernel,
        out_shape=jax.ShapeDtypeStruct((GROUPS * 8, BN, AN), BF),
        in_specs=[
            pl.BlockSpec(memory_space=pltpu.SMEM),
            pl.BlockSpec(memory_space=vmem),
            pl.BlockSpec(memory_space=vmem),
            pl.BlockSpec(memory_space=pl.ANY),
        ],
        out_specs=pl.BlockSpec(memory_space=vmem),
        scratch_shapes=[
            vmem((CB, QN, AN), BF),
            vmem((CB * AN, QN), BF),
            vmem((GROUPS, ROWS * SECTS, CB * DN), BF),
            vmem((QN, BN, DN), BF),
            vmem((BN, QN, DN), BF),
            vmem((BN, AN, CB * DN), BF),
            vmem(whole + (2, XN, ZN, NB) + spot, F32),
            vmem(whole + (2, XN, ZN, NB) + spot, BF),
            vmem(whole + (XN, ZN, NB) + spot, BF),
            vmem(whole + (XN, ZN, NB) + spot, F32),
            vmem(whole + (XN, ZN, NB) + spot, BF),
            vmem(whole + (2, ZN // 2, NB) + spot, BF),
            vmem(whole + (2, ZN // 2, NB) + spot, BF),
            vmem(whole + (2, ZN, NB) + spot, BF),
            vmem(whole + (ZN, NB) + spot, F32),
            vmem(whole + (ZN, NB) + spot, BF),
            vmem(whole + (2, NB // 2) + spot, BF),
            vmem(whole + (2, NB // 2) + spot, BF),
            vmem(whole + (2, NB) + spot, BF),
            vmem((GROUPS, RC * NB) + spot, F32),
            vmem((BN // 4, ROWS * SECTS, 4 * AN), F32),
            dma((STAGES,)),
            dma((16, 7)),
            dma((16, SECTS)),
            dma(whole),
            dma(whole),
            dma(whole + (6,)),
            dma(whole + (6,)),
            dma(whole + (6,)),
            dma(whole + (6,)),
        ],
        compiler_params=pltpu.CompilerParams(
            collective_id=0, has_side_effects=True, vmem_limit_bytes=56 << 20
        ),
        cost_estimate=pl.CostEstimate(flops=12_000_000_000, bytes_accessed=8_000_000, transcendentals=0),
    )(irrep_counts, chol_left, lam, chol_right)
    return jnp.transpose(summed, (0, 2, 1))


def solution(mesh):
    return jax.shard_map(
        per_device,
        mesh=mesh,
        in_specs=(P(), P("sect", "tile", None), P(None, "sect", None), P("sect", "tile", None)),
        out_specs=P("tile", None, "sect"),
        check_vma=False,
    )
```

```python
import functools

import jax
import jax.numpy as jnp
from jax import lax
from jax.experimental import pallas as pl
from jax.experimental.pallas import tpu as pltpu
from jax.sharding import PartitionSpec as P

MESH = pl.DeviceIdType.MESH
BF, F32 = jnp.bfloat16, jnp.float32
YN, XN, ZN = 4, 4, 4
SECTS = 2 * YN
QB, CB, AN, DN = 112, 8, 128, 256
QN = QB * SECTS
BN = 16
GROUPS, ROWS = 2, 32
BLOCK = 4
RC, NB = 2, 4
STAGES = 14
STEP = QN // STAGES
Z_FIRST = (0, 0, 0, 1, 1, 1, 1, 0, 1, 0, 0, 1, 0, 1, 1, 1)
FAR_PLUS = (0, 1, 0, 1, 1, 1, 0, 0, 1, 1, 0, 1, 0, 1, 1, 0)


def kernel(counts, left, lam, right, out,
           lbuf, ltra, ltrb, ltr, mbuf, rstage, rmat, coul, p32, pbf, rpair,
           s32, sbf, xfar, xfwd, xdir, u32, ubf, zfar, zfwd, zdir,
           v32, acc, acc0, rsem, ag_send, ag_recv, pr_send, pr_recv, x_send, x_recv, z_send, z_recv):
    sect, tile = lax.axis_index("sect"), lax.axis_index("tile")
    zl, y = sect // YN, sect % YN
    zh, x, core = tile // (2 * XN), (tile // 2) % XN, tile % 2
    base, obase = zl * YN, (1 - zl) * YN
    yp, ym, yf = (y + 1) % YN, (y + YN - 1) % YN, (y + 2) % YN
    at_yp, at_ym, at_z = {"sect": base + yp}, {"sect": base + ym}, {"sect": obase + y}

    bm, bp, bf = base + ym, base + yp, base + yf
    oy, om, op, of = obase + y, obase + ym, obase + yp, obase + yf

    def tile_at(zz, xx, cc):
        return {"tile": (zz * XN + xx) * 2 + cc}

    xp, xm, xf = (x + 1) % XN, (x + XN - 1) % XN, (x + 2) % XN
    zp, zm, zf = (zh + 1) % ZN, (zh + ZN - 1) % ZN, (zh + 2) % ZN
    at_xp, at_xm = tile_at(zh, xp, core), tile_at(zh, xm, core)
    at_zp, at_zm = tile_at(zp, x, core), tile_at(zm, x, core)
    at_pair = tile_at(zh, x, 1 - core)

    barrier = pltpu.get_barrier_semaphore()
    friends = (at_yp, at_ym, at_z, at_xp, at_xm, at_zp, at_zm, at_pair)
    for friend in friends:
        pl.semaphore_signal(barrier, inc=1, device_id=friend, device_id_type=MESH)

    def stage_copy(k):
        rows = pl.ds(k * STEP, STEP)
        return pltpu.make_async_copy(right.at[rows], rstage.at[rows], rsem.at[k])

    for k in range(STAGES):
        stage_copy(k).start()

    n1, n2 = counts[0], counts[1]
    own = pltpu.einshape("qca->cqa", left[...])
    lane = lax.broadcasted_iota(jnp.int32, (QB, AN), 1)
    for c in range(CB):
        orbital = tile * CB + c
        room = jnp.where(orbital < AN, n1 - orbital, n2 + AN - orbital)
        limit = jnp.where(room > 0, n1, 0)
        kept = jnp.where(lane < limit, own[c].astype(F32), 0.0).astype(BF)
        lbuf[c, pl.ds(pl.multiple_of(sect * QB, 16), QB), :] = kept
    lane = lax.broadcasted_iota(jnp.int32, (ROWS, DN), 1)
    d_live = lane < jnp.where(lane < AN, n1, n2 + AN)
    for g in range(GROUPS):
        mine = jnp.concatenate([lam[16 * u + 8 * g : 16 * u + 8 * g + 8] for u in range(4)], axis=0)
        mine = pltpu.einshape("icd->cid", mine)
        for c in range(CB):
            kept = jnp.where(d_live, mine[c].astype(F32), 0.0).astype(BF)
            mbuf[g, pl.ds(pl.multiple_of(sect * ROWS, 16), ROWS), c * DN : (c + 1) * DN] = kept

    sent = []

    def go(make):
        make().start()
        sent.append(make)

    def piece(p, src):
        if p < 8:
            return lbuf.at[p, pl.ds(pl.multiple_of(src * QB, 16), QB), :]
        g, part = divmod(p - 8, 4)
        return mbuf.at[g, pl.ds(pl.multiple_of(src * ROWS, 16), ROWS), pl.ds(part * 2 * DN, 2 * DN)]

    def pass_on(p, src, k, where):
        def make():
            ref = piece(p, src)
            return pltpu.make_async_remote_copy(ref, ref, ag_send.at[p, k], ag_recv.at[p, src], where, MESH)

        go(make)

    def arrived(p, src):
        ref = piece(p, src)
        pltpu.make_async_remote_copy(ref, ref, ag_send.at[p, 0], ag_recv.at[p, src], at_z, MESH).wait_recv()

    def ag_own(p):
        if Z_FIRST[p]:
            pass_on(p, sect, 0, at_z)
        pass_on(p, sect, 1, at_yp)
        pass_on(p, sect, 2, at_ym)
        if not Z_FIRST[p]:
            pass_on(p, sect, 0, at_z)

    def ag_near(p):
        if Z_FIRST[p]:
            arrived(p, oy)
            pass_on(p, oy, 4, at_yp)
            pass_on(p, oy, 5, at_ym)
        arrived(p, bm)
        if FAR_PLUS[p]:
            pass_on(p, bm, 3, at_yp)
        if not Z_FIRST[p]:
            pass_on(p, bm, 4, at_z)
        arrived(p, bp)
        if not FAR_PLUS[p]:
            pass_on(p, bp, 3, at_ym)
        if not Z_FIRST[p]:
            pass_on(p, bp, 5, at_z)

    def ag_far(p):
        if Z_FIRST[p]:
            arrived(p, om)
            if FAR_PLUS[p]:
                pass_on(p, om, 6, at_yp)
            arrived(p, op)
            if not FAR_PLUS[p]:
                pass_on(p, op, 6, at_ym)
        else:
            arrived(p, bf)
            pass_on(p, bf, 6, at_z)

    def ag_half(p):
        if Z_FIRST[p]:
            arrived(p, bf)

    def ag_end(p):
        if Z_FIRST[p]:
            if p >= 4:
                arrived(p, bf)
            arrived(p, of)
        else:
            for src in (oy, om, op, of):
                arrived(p, src)

    def run(*todo):
        for event in todo:
            event()

    def loop(count, body, events):
        def step(j, carry):
            body(j)
            for k, todo in events.items():
                pl.when(j == k)(functools.partial(run, *todo))
            return carry

        lax.fori_loop(0, count, step, 0)

    def relay(events):
        def body(k):
            stage_copy(k).wait()
            rows = pl.ds(pl.multiple_of(k * STEP, 16), STEP)
            rmat[:, rows, :] = pltpu.einshape("qbd->bqd", rstage[rows])

        loop(STAGES, body, events)

    def layer(which):
        return pl.ds(pl.multiple_of(which * (QN // 2), 16), QN // 2)

    def turn_a():
        for c in range(4):
            ltra[c * AN : (c + 1) * AN, :] = lbuf[c, layer(zl), :].T

    def turn_b():
        for c in range(4):
            ltrb[c * AN : (c + 1) * AN, :] = lbuf[c, layer(1 - zl), :].T

    def turn_1():
        for c in range(4):
            ltr[c * AN : (c + 1) * AN, :] = lbuf[4 + c].T

    def keep(b, first, block):
        for k in range(4):
            c = first + k
            coul[b, :, c * DN : (c + 1) * DN] = block[k * AN : (k + 1) * AN].astype(BF)

    def coulomb_a(events):
        def body(j):
            for k in range(BLOCK):
                b = BLOCK * j + k
                acc0[b] = jnp.dot(ltra[...], rmat[b, layer(zl), :], preferred_element_type=F32)

        loop(BN // BLOCK, body, events)

    def coulomb_b(events):
        def body(j):
            for k in range(BLOCK):
                b = BLOCK * j + k
                keep(b, 0, acc0[b] + jnp.dot(ltrb[...], rmat[b, layer(1 - zl), :], preferred_element_type=F32))

        loop(BN // BLOCK, body, events)

    def coulomb_1(events):
        def body(j):
            for k in range(BLOCK):
                b = BLOCK * j + k
                keep(b, 4, jnp.dot(ltr[...], rmat[b], preferred_element_type=F32))

        loop(BN // BLOCK, body, events)

    def product(g, quad, first, last):
        cols = coul[4 * quad : 4 * quad + 4, :, first * DN : last * DN].reshape(4 * AN, (last - first) * DN)
        rows = mbuf[g, :, first * DN : last * DN]
        return lax.dot_general(rows, cols, (((1,), (1,)), ((), ())), preferred_element_type=F32)

    def early():
        for quad in range(BN // 4):
            acc[quad] = product(1, quad, 0, CB // 2)

    def ladder(g, r):
        for k in range(NB // 2):
            quad = r * (NB // 2) + k
            block = product(g, quad, 0, CB) if g == 0 else acc[quad] + product(g, quad, CB // 2, CB)
            for m in range(2):
                part = block[:, 2 * AN * m : 2 * AN * (m + 1)].reshape(ZN, XN, 2, 8, 2 * AN)
                part = jnp.concatenate([part[..., :AN], part[..., AN:]], axis=3)
                for cc in range(2):
                    for xx in range(XN):
                        p32[g, r, cc, xx, :, 2 * k + m] = part[:, xx, cc]
                        pbf[g, r, cc, xx, :, 2 * k + m] = part[:, xx, cc].astype(BF)

    def pair_copy(g, r):
        return pltpu.make_async_remote_copy(
            pbf.at[g, r, 1 - core], rpair.at[g, r], pr_send.at[g, r], pr_recv.at[g, r], at_pair, MESH)

    def ring_copies(g, r, bf, far, fwd, direct, sends, recvs, cp, cm, cf, to_p, to_m):
        half = bf.shape[3] // 2
        lo, hi = pl.ds(0, half), pl.ds(half, half)
        ends = (
            (bf.at[g, r, cf, lo], far.at[g, r, 0], to_p),
            (bf.at[g, r, cf, hi], far.at[g, r, 1], to_m),
            (bf.at[g, r, cp, hi], direct.at[g, r, 0, hi], to_p),
            (bf.at[g, r, cm, lo], direct.at[g, r, 1, lo], to_m),
            (fwd.at[g, r, 0], direct.at[g, r, 0, lo], to_p),
            (fwd.at[g, r, 1], direct.at[g, r, 1, hi], to_m),
        )

        def copy(k):
            src, dst, where = ends[k]
            return pltpu.make_async_remote_copy(src, dst, sends.at[g, r, k], recvs.at[g, r, k], where, MESH)

        return copy

    def x_copies(g, r):
        return ring_copies(g, r, sbf, xfar, xfwd, xdir, x_send, x_recv, xp, xm, xf, at_xp, at_xm)

    def z_copies(g, r):
        return ring_copies(g, r, ubf, zfar, zfwd, zdir, z_send, z_recv, zp, zm, zf, at_zp, at_zm)

    def ring_mid(g, r, ring, total, far, fwd, cp, cm):
        half = total.shape[3] // 2
        copies = ring(g, r)
        copies(0).wait_recv()
        fwd[g, r, 0] = (total[g, r, cp, :half] + far[g, r, 0].astype(F32)).astype(BF)
        go(lambda: ring(g, r)(4))
        copies(1).wait_recv()
        fwd[g, r, 1] = (total[g, r, cm, half:] + far[g, r, 1].astype(F32)).astype(BF)
        go(lambda: ring(g, r)(5))

    def ring_end(g, r, copies, total, direct, me):
        for k in range(2, 6):
            copies(k).wait_recv()
        return total[g, r, me] + direct[g, r, 0].astype(F32) + direct[g, r, 1].astype(F32)

    def red1(g, r):
        go(functools.partial(pair_copy, g, r))

    def red2(g, r):
        pair_copy(g, r).wait_recv()
        for xx in range(XN):
            total = p32[g, r, core, xx] + rpair[g, r, xx].astype(F32)
            s32[g, r, xx] = total
            sbf[g, r, xx] = total.astype(BF)
        for k in range(4):
            go(functools.partial(lambda k: x_copies(g, r)(k), k))

    def red3(g, r):
        ring_mid(g, r, x_copies, s32, xfar, xfwd, xp, xm)

    def red4(g, r):
        total = ring_end(g, r, x_copies(g, r), s32, xdir, x)
        u32[g, r] = total
        ubf[g, r] = total.astype(BF)
        for k in range(4):
            go(functools.partial(lambda k: z_copies(g, r)(k), k))

    def red5(g, r):
        ring_mid(g, r, z_copies, u32, zfar, zfwd, zp, zm)

    def red6(g, r):
        v32[g, r * NB : (r + 1) * NB] = ring_end(g, r, z_copies(g, r), u32, zdir, zh)

    def finish(g):
        summed = pltpu.einshape("bia->iba", v32[g].reshape(BN, 8, AN))
        orbital = sect * BN + lax.broadcasted_iota(jnp.int32, summed.shape, 1)
        out[8 * g : 8 * g + 8] = jnp.where(orbital < n2, summed, 0.0).astype(BF)

    pieces, chunks = range(16), [(g, r) for g in range(GROUPS) for r in range(RC)]
    o, n, f, e, h = ([functools.partial(act, p) for p in pieces] for act in (ag_own, ag_near, ag_far, ag_end, ag_half))
    r1, r2, r3, r4, r5, r6 = (
        {at: functools.partial(act, *at) for at in chunks} for act in (red1, red2, red3, red4, red5, red6)
    )

    pl.semaphore_wait(barrier, len(friends))

    run(o[0], o[1], o[2], o[3], o[4], o[5])
    relay({7: (n[0], o[6], n[1],), 9: (n[2], o[7],), 10: (n[3],), 11: (n[4],)})
    run(n[5], f[0], f[1], o[8], f[2], n[6], n[7], h[0], h[1], h[2], h[3])
    turn_a()
    run(f[3])
    coulomb_a({0: (f[4], o[9],), 1: (o[10], f[5],), 2: (o[11],)})
    run(o[12], f[6], f[7], n[8], e[0], e[1], e[2], e[3])
    turn_b()
    coulomb_b({0: (n[9], o[13], n[10],), 2: (o[14], n[11], n[12], f[8],)})
    run(e[4], e[5], e[6], e[7])
    turn_1()
    run(o[15], f[9], f[10])
    coulomb_1({0: (n[13],), 1: (f[11], f[12], n[14],), 2: (n[15], f[13],)})
    run(e[8], e[9], e[10], e[11])
    ladder(0, 0)
    run(r1[0, 0], f[14])
    ladder(0, 1)
    run(r1[0, 1], f[15], r2[0, 0], e[12], e[13])
    early()
    run(r2[0, 1], e[14], e[15])
    ladder(1, 0)
    run(r1[1, 0], r3[0, 0])
    ladder(1, 1)
    run(r1[1, 1], r3[0, 1], r2[1, 0], r2[1, 1], r4[0, 0], r4[0, 1], r3[1, 0], r3[1, 1], r5[0, 0], r5[0, 1], r4[1, 0], r4[1, 1], r6[0, 0], r6[0, 1], r5[1, 0], r5[1, 1], r6[1, 0], r6[1, 1])
    finish(0)
    finish(1)
    for make in sent:
        make().wait_send()


def per_device(irrep_counts, chol_left, chol_right, lam):
    whole = (GROUPS, RC)
    spot = (16, AN)
    vmem = pltpu.VMEM
    dma = pltpu.SemaphoreType.DMA
    summed = pl.pallas_call(
        kernel,
        out_shape=jax.ShapeDtypeStruct((GROUPS * 8, BN, AN), BF),
        in_specs=[
            pl.BlockSpec(memory_space=pltpu.SMEM),
            pl.BlockSpec(memory_space=vmem),
            pl.BlockSpec(memory_space=vmem),
            pl.BlockSpec(memory_space=pl.ANY),
        ],
        out_specs=pl.BlockSpec(memory_space=vmem),
        scratch_shapes=[
            vmem((CB, QN, AN), BF),
            vmem((4 * AN, QN // 2), BF),
            vmem((4 * AN, QN // 2), BF),
            vmem((4 * AN, QN), BF),
            vmem((GROUPS, ROWS * SECTS, CB * DN), BF),
            vmem((QN, BN, DN), BF),
            vmem((BN, QN, DN), BF),
            vmem((BN, AN, CB * DN), BF),
            vmem(whole + (2, XN, ZN, NB) + spot, F32),
            vmem(whole + (2, XN, ZN, NB) + spot, BF),
            vmem(whole + (XN, ZN, NB) + spot, BF),
            vmem(whole + (XN, ZN, NB) + spot, F32),
            vmem(whole + (XN, ZN, NB) + spot, BF),
            vmem(whole + (2, ZN // 2, NB) + spot, BF),
            vmem(whole + (2, ZN // 2, NB) + spot, BF),
            vmem(whole + (2, ZN, NB) + spot, BF),
            vmem(whole + (ZN, NB) + spot, F32),
            vmem(whole + (ZN, NB) + spot, BF),
            vmem(whole + (2, NB // 2) + spot, BF),
            vmem(whole + (2, NB // 2) + spot, BF),
            vmem(whole + (2, NB) + spot, BF),
            vmem((GROUPS, RC * NB) + spot, F32),
            vmem((BN // 4, ROWS * SECTS, 4 * AN), F32),
            vmem((BN, 4 * AN, DN), F32),
            dma((STAGES,)),
            dma((16, 7)),
            dma((16, SECTS)),
            dma(whole),
            dma(whole),
            dma(whole + (6,)),
            dma(whole + (6,)),
            dma(whole + (6,)),
            dma(whole + (6,)),
        ],
        compiler_params=pltpu.CompilerParams(
            collective_id=0, has_side_effects=True, vmem_limit_bytes=56 << 20
        ),
        cost_estimate=pl.CostEstimate(flops=12_000_000_000, bytes_accessed=8_000_000, transcendentals=0),
    )(irrep_counts, chol_left, lam, chol_right)
    return jnp.transpose(summed, (0, 2, 1))


def solution(mesh):
    return jax.shard_map(
        per_device,
        mesh=mesh,
        in_specs=(P(), P("sect", "tile", None), P(None, "sect", None), P("sect", "tile", None)),
        out_specs=P("tile", None, "sect"),
        check_vma=False,
    )
```

```python
import functools

import jax
import jax.numpy as jnp
from jax import lax
from jax.experimental import pallas as pl
from jax.experimental.pallas import tpu as pltpu
from jax.sharding import PartitionSpec as P

MESH = pl.DeviceIdType.MESH
BF, F32 = jnp.bfloat16, jnp.float32
YN, XN, ZN = 4, 4, 4
SECTS = 2 * YN
QB, CB, AN, DN = 112, 8, 128, 256
QN = QB * SECTS
BN = 16
GROUPS, ROWS = 2, 32
BLOCK = 4
CHUNKS = ((0, 0, 4), (0, 4, 4), (1, 0, 2), (1, 2, 2), (1, 4, 2), (1, 6, 2))
Z_LEADS = (0, 0, 0, 1, 0, 0)
STAGES = 14
STEP = QN // STAGES
Z_FIRST = (0, 1, 0, 1, 0, 1, 1, 0, 1, 0, 1, 0, 1, 0, 1, 0)
FAR_PLUS = (1, 1, 0, 0, 1, 1, 1, 1, 0, 0, 1, 0, 1, 0, 1, 0)


def kernel(counts, left, lam, right, out,
           lbuf, ltra, ltrb, ltr, mbuf, rstage, rmat, coul, p32, pbf, rpair,
           s32, sbf, xdir, u32, ubf, zdir,
           v32, acc, acc0, lown, mown, in_sem, rsem, ag_send, ag_recv, hello, pr_send, pr_recv, x_send, x_recv, z_send, z_recv):
    sect, tile = lax.axis_index("sect"), lax.axis_index("tile")
    zl, y = sect // YN, sect % YN
    zh, x, core = tile // (2 * XN), (tile // 2) % XN, tile % 2
    base, obase = zl * YN, (1 - zl) * YN
    yp, ym, yf = (y + 1) % YN, (y + YN - 1) % YN, (y + 2) % YN
    at_yp, at_ym, at_z = {"sect": base + yp}, {"sect": base + ym}, {"sect": obase + y}

    bm, bp, bf = base + ym, base + yp, base + yf
    oy, om, op, of = obase + y, obase + ym, obase + yp, obase + yf

    def tile_at(zz, xx, cc):
        return {"tile": (zz * XN + xx) * 2 + cc}

    xp, xm, xf = (x + 1) % XN, (x + XN - 1) % XN, (x + 2) % XN
    zp, zm, zf = (zh + 1) % ZN, (zh + ZN - 1) % ZN, (zh + 2) % ZN
    at_xp, at_xm = tile_at(zh, xp, core), tile_at(zh, xm, core)
    at_zp, at_zm = tile_at(zp, x, core), tile_at(zm, x, core)
    at_xf, at_zf = tile_at(zh, xf, core), tile_at(zf, x, core)
    at_pair = tile_at(zh, x, 1 - core)

    barrier = pltpu.get_barrier_semaphore()
    friends = (at_yp, at_ym, at_z, at_xp, at_xm, at_zp, at_zm, at_pair)
    for friend in friends:
        pl.semaphore_signal(barrier, inc=1, device_id=friend, device_id_type=MESH)

    def stage_copy(k):
        rows = pl.ds(k * STEP, STEP)
        return pltpu.make_async_copy(right.at[rows], rstage.at[rows], rsem.at[k])

    pltpu.make_async_copy(left, lown, in_sem.at[0]).start()
    pltpu.make_async_copy(lam, mown, in_sem.at[1]).start()
    for k in range(STAGES):
        stage_copy(k).start()

    n1, n2 = counts[0], counts[1]
    left_copy = pltpu.make_async_copy(left, lown, in_sem.at[0])
    lam_copy = pltpu.make_async_copy(lam, mown, in_sem.at[1])
    left_copy.wait()
    own = pltpu.einshape("qca->cqa", lown[...])
    lane = lax.broadcasted_iota(jnp.int32, (QB, AN), 1)
    for c in range(CB):
        orbital = tile * CB + c
        room = jnp.where(orbital < AN, n1 - orbital, n2 + AN - orbital)
        limit = jnp.where(room > 0, n1, 0)
        kept = jnp.where(lane < limit, own[c].astype(F32), 0.0).astype(BF)
        lbuf[c, pl.ds(pl.multiple_of(sect * QB, 16), QB), :] = kept
    lane = lax.broadcasted_iota(jnp.int32, (ROWS, DN), 1)
    d_live = lane < jnp.where(lane < AN, n1, n2 + AN)
    lam_copy.wait()
    for g in range(GROUPS):
        mine = jnp.concatenate([mown[16 * u + 8 * g : 16 * u + 8 * g + 8] for u in range(4)], axis=0)
        mine = pltpu.einshape("icd->cid", mine)
        for c in range(CB):
            kept = jnp.where(d_live, mine[c].astype(F32), 0.0).astype(BF)
            mbuf[g, pl.ds(pl.multiple_of(sect * ROWS, 16), ROWS), c * DN : (c + 1) * DN] = kept

    sent = []

    def go(make):
        make().start()
        sent.append(make)

    def piece(p, src):
        if p < 8:
            return lbuf.at[p, pl.ds(pl.multiple_of(src * QB, 16), QB), :]
        g, part = divmod(p - 8, 4)
        return mbuf.at[g, pl.ds(pl.multiple_of(src * ROWS, 16), ROWS), pl.ds(part * 2 * DN, 2 * DN)]

    def pass_on(p, src, k, where):
        def make():
            ref = piece(p, src)
            return pltpu.make_async_remote_copy(ref, ref, ag_send.at[p, k], ag_recv.at[p, src], where, MESH)

        go(make)

    def arrived(p, src):
        ref = piece(p, src)
        pltpu.make_async_remote_copy(ref, ref, ag_send.at[p, 0], ag_recv.at[p, src], at_z, MESH).wait_recv()

    def ag_own(p):
        if Z_FIRST[p]:
            pass_on(p, sect, 0, at_z)
        pass_on(p, sect, 1, at_yp)
        pass_on(p, sect, 2, at_ym)
        if not Z_FIRST[p]:
            pass_on(p, sect, 0, at_z)

    def ag_near(p):
        if Z_FIRST[p]:
            arrived(p, oy)
            pass_on(p, oy, 4, at_yp)
            pass_on(p, oy, 5, at_ym)
        arrived(p, bm)
        if FAR_PLUS[p]:
            pass_on(p, bm, 3, at_yp)
        if not Z_FIRST[p]:
            pass_on(p, bm, 4, at_z)
        arrived(p, bp)
        if not FAR_PLUS[p]:
            pass_on(p, bp, 3, at_ym)
        if not Z_FIRST[p]:
            pass_on(p, bp, 5, at_z)

    def ag_far(p):
        if Z_FIRST[p]:
            arrived(p, om)
            if FAR_PLUS[p]:
                pass_on(p, om, 6, at_yp)
            arrived(p, op)
            if not FAR_PLUS[p]:
                pass_on(p, op, 6, at_ym)
        else:
            arrived(p, bf)
            pass_on(p, bf, 6, at_z)

    def ag_half(p):
        if Z_FIRST[p]:
            arrived(p, bf)

    def ag_end(p):
        if Z_FIRST[p]:
            if p >= 4:
                arrived(p, bf)
            arrived(p, of)
        else:
            for src in (oy, om, op, of):
                arrived(p, src)

    def run(*todo):
        for event in todo:
            event()

    def loop(count, body, events):
        def step(j, carry):
            body(j)
            for k, todo in events.items():
                pl.when(j == k)(functools.partial(run, *todo))
            return carry

        lax.fori_loop(0, count, step, 0)

    def relay(events):
        def body(k):
            stage_copy(k).wait()
            rows = pl.ds(pl.multiple_of(k * STEP, 16), STEP)
            rmat[:, rows, :] = pltpu.einshape("qbd->bqd", rstage[rows])

        loop(STAGES, body, events)

    def layer(which):
        return pl.ds(pl.multiple_of(which * (QN // 2), 16), QN // 2)

    def turn_a():
        for c in range(4):
            ltra[c * AN : (c + 1) * AN, :] = lbuf[c, layer(zl), :].T

    def turn_b():
        for c in range(4):
            ltrb[c * AN : (c + 1) * AN, :] = lbuf[c, layer(1 - zl), :].T

    def turn_1():
        for c in range(4):
            ltr[c * AN : (c + 1) * AN, :] = lbuf[4 + c].T

    def keep(b, first, block):
        for k in range(4):
            c = first + k
            coul[b, :, c * DN : (c + 1) * DN] = block[k * AN : (k + 1) * AN].astype(BF)

    def coulomb_a(events):
        def body(j):
            for k in range(BLOCK):
                b = BLOCK * j + k
                acc0[b] = jnp.dot(ltra[...], rmat[b, layer(zl), :], preferred_element_type=F32)

        loop(BN // BLOCK, body, events)

    def coulomb_b(events):
        def body(j):
            for k in range(BLOCK):
                b = BLOCK * j + k
                keep(b, 0, acc0[b] + jnp.dot(ltrb[...], rmat[b, layer(1 - zl), :], preferred_element_type=F32))

        loop(BN // BLOCK, body, events)

    def coulomb_1(events):
        def body(j):
            for k in range(BLOCK):
                b = BLOCK * j + k
                keep(b, 4, jnp.dot(ltr[...], rmat[b], preferred_element_type=F32))

        loop(BN // BLOCK, body, events)

    def product(g, quad, first, last):
        cols = coul[4 * quad : 4 * quad + 4, :, first * DN : last * DN].reshape(4 * AN, (last - first) * DN)
        rows = mbuf[g, :, first * DN : last * DN]
        return lax.dot_general(rows, cols, (((1,), (1,)), ((), ())), preferred_element_type=F32)

    def early():
        for quad in range(BN // 4):
            acc[quad] = product(1, quad, 0, CB // 2)

    def ladder(t):
        g, first, count = CHUNKS[t]
        for quad in range(first // 2, (first + count) // 2):
            block = product(g, quad, 0, CB) if g == 0 else acc[quad] + product(g, quad, CB // 2, CB)
            for m in range(2):
                part = block[:, 2 * AN * m : 2 * AN * (m + 1)].reshape(ZN, XN, 2, 8, 2 * AN)
                part = jnp.concatenate([part[..., :AN], part[..., AN:]], axis=3)
                for cc in range(2):
                    for xx in range(XN):
                        p32[g, cc, xx, :, 2 * quad + m] = part[:, xx, cc]
                        pbf[g, cc, xx, :, 2 * quad + m] = part[:, xx, cc].astype(BF)

    def part_of(t):
        g, first, count = CHUNKS[t]
        return g, pl.ds(first, count)

    def pair_copy(t):
        g, js = part_of(t)
        return pltpu.make_async_remote_copy(
            pbf.at[g, 1 - core, :, :, js], rpair.at[g, :, :, js], pr_send.at[t], pr_recv.at[t], at_pair, MESH)

    x_ends, z_ends = ((xf, at_xf), (xp, at_xp), (xm, at_xm)), ((zf, at_zf), (zp, at_zp), (zm, at_zm))

    def first_copies(t, k):
        g, js = part_of(t)
        to, where = (z_ends if Z_LEADS[t] else x_ends)[k]
        src = sbf.at[g, :, to, js] if Z_LEADS[t] else sbf.at[g, to, :, js]
        return pltpu.make_async_remote_copy(src, xdir.at[g, k, :, js], x_send.at[t, k], x_recv.at[t, k], where, MESH)

    def last_copies(t, k):
        g, js = part_of(t)
        to, where = (x_ends if Z_LEADS[t] else z_ends)[k]
        return pltpu.make_async_remote_copy(
            ubf.at[g, to, js], zdir.at[g, k, js], z_send.at[t, k], z_recv.at[t, k], where, MESH)

    def red1(t):
        go(functools.partial(pair_copy, t))

    def red2(t):
        g, js = part_of(t)
        pair_copy(t).wait_recv()
        for xx in range(XN):
            total = p32[g, core, xx, :, js] + rpair[g, xx, :, js].astype(F32)
            s32[g, xx, :, js] = total
            sbf[g, xx, :, js] = total.astype(BF)
        for k in range(3):
            go(functools.partial(first_copies, t, k))

    def red4(t):
        g, js = part_of(t)
        for k in range(3):
            first_copies(t, k).wait_recv()
        total = s32[g, :, zh, js] if Z_LEADS[t] else s32[g, x, :, js]
        for k in range(3):
            total = total + xdir[g, k, :, js].astype(F32)
        u32[g, :, js] = total
        ubf[g, :, js] = total.astype(BF)
        for k in range(3):
            go(functools.partial(last_copies, t, k))

    def red6(t):
        g, js = part_of(t)
        for k in range(3):
            last_copies(t, k).wait_recv()
        total = u32[g, x if Z_LEADS[t] else zh, js]
        for k in range(3):
            total = total + zdir[g, k, js].astype(F32)
        v32[g, js] = total

    def greet():
        pl.semaphore_wait(hello, 4)

    def finish(g):
        summed = pltpu.einshape("bia->iba", v32[g].reshape(BN, 8, AN))
        orbital = sect * BN + lax.broadcasted_iota(jnp.int32, summed.shape, 1)
        out[8 * g : 8 * g + 8] = jnp.where(orbital < n2, summed, 0.0).astype(BF)

    o, n, f, e, h = ([functools.partial(act, p) for p in range(16)] for act in (ag_own, ag_near, ag_far, ag_end, ag_half))
    r1, r2, r4, r6 = ([functools.partial(act, t) for t in range(len(CHUNKS))] for act in (red1, red2, red4, red6))

    pl.semaphore_wait(barrier, len(friends))
    for friend in (at_xp, at_xm, at_zp, at_zm):
        pl.semaphore_signal(hello, inc=1, device_id=friend, device_id_type=MESH)

    run(o[0], o[1], o[2], o[3], o[4], o[5])
    relay({8: (o[6], n[0],), 9: (o[7], n[1], n[2],), 11: (n[3],), 12: (n[4],)})
    run(n[5], n[6], f[0], n[7], o[8], f[1], f[2], o[9], h[0], h[1], h[2], h[3])
    turn_a()
    run(o[10], f[3])
    coulomb_a({0: (f[4], o[11], f[5],), 1: (o[12], f[6],), 2: (o[13], f[7],)})
    run(o[14], n[8], e[0], e[1], e[2], e[3])
    turn_b()
    coulomb_b({0: (n[9], n[10],), 1: (n[11],), 2: (n[12],)})
    run(e[4], e[5], e[6], e[7])
    turn_1()
    run(o[15], n[13], n[14], f[9])
    coulomb_1({0: (f[8], f[10], f[11],), 1: (f[12],), 2: (f[13], n[15], f[14],)})
    run(e[8], e[9], e[10], e[11])
    ladder(0)
    run(r1[0])
    ladder(1)
    run(r1[1], f[15], greet, r2[0], e[12], e[13])
    early()
    run(r2[1], e[14], e[15])
    ladder(2)
    run(r1[2])
    ladder(3)
    run(r1[3])
    ladder(4)
    run(r1[4], r4[0], r2[2], r2[3])
    ladder(5)
    run(r1[5], r2[4], r4[1], r2[5], r4[2], r6[0], r4[4], r4[5], r4[3], r6[1], r6[2], r6[3], r6[4], r6[5])
    finish(0)
    finish(1)
    for make in sent:
        make().wait_send()


def per_device(irrep_counts, chol_left, chol_right, lam):
    spot = (BN // 2, 16, AN)
    vmem = pltpu.VMEM
    dma = pltpu.SemaphoreType.DMA
    summed = pl.pallas_call(
        kernel,
        out_shape=jax.ShapeDtypeStruct((GROUPS * 8, BN, AN), BF),
        in_specs=[
            pl.BlockSpec(memory_space=pltpu.SMEM),
            pl.BlockSpec(memory_space=pl.ANY),
            pl.BlockSpec(memory_space=pl.ANY),
            pl.BlockSpec(memory_space=pl.ANY),
        ],
        out_specs=pl.BlockSpec(memory_space=vmem),
        scratch_shapes=[
            vmem((CB, QN, AN), BF),
            vmem((4 * AN, QN // 2), BF),
            vmem((4 * AN, QN // 2), BF),
            vmem((4 * AN, QN), BF),
            vmem((GROUPS, ROWS * SECTS, CB * DN), BF),
            vmem((QN, BN, DN), BF),
            vmem((BN, QN, DN), BF),
            vmem((BN, AN, CB * DN), BF),
            vmem((GROUPS, 2, XN, ZN) + spot, F32),
            vmem((GROUPS, 2, XN, ZN) + spot, BF),
            vmem((GROUPS, XN, ZN) + spot, BF),
            vmem((GROUPS, XN, ZN) + spot, F32),
            vmem((GROUPS, XN, ZN) + spot, BF),
            vmem((GROUPS, 3, ZN) + spot, BF),
            vmem((GROUPS, ZN) + spot, F32),
            vmem((GROUPS, ZN) + spot, BF),
            vmem((GROUPS, 3) + spot, BF),
            vmem((GROUPS,) + spot, F32),
            vmem((BN // 4, ROWS * SECTS, 4 * AN), F32),
            vmem((BN, 4 * AN, DN), F32),
            vmem((QB, CB, AN), BF),
            vmem((SECTS * 8, CB, DN), BF),
            dma((2,)),
            dma((STAGES,)),
            dma((16, 7)),
            dma((16, SECTS)),
            pltpu.SemaphoreType.REGULAR,
            dma((len(CHUNKS),)),
            dma((len(CHUNKS),)),
            dma((len(CHUNKS), 3)),
            dma((len(CHUNKS), 3)),
            dma((len(CHUNKS), 3)),
            dma((len(CHUNKS), 3)),
        ],
        compiler_params=pltpu.CompilerParams(
            collective_id=0, has_side_effects=True, vmem_limit_bytes=56 << 20
        ),
        cost_estimate=pl.CostEstimate(flops=12_000_000_000, bytes_accessed=8_000_000, transcendentals=0),
    )(irrep_counts, chol_left, lam, chol_right)
    return jnp.transpose(summed, (0, 2, 1))


def solution(mesh):
    return jax.shard_map(
        per_device,
        mesh=mesh,
        in_specs=(P(), P("sect", "tile", None), P(None, "sect", None), P("sect", "tile", None)),
        out_specs=P("tile", None, "sect"),
        check_vma=False,
    )
```

```python
import functools

import jax
import jax.numpy as jnp
from jax import lax
from jax.experimental import pallas as pl
from jax.experimental.pallas import tpu as pltpu
from jax.sharding import PartitionSpec as P

MESH = pl.DeviceIdType.MESH
BF, F32 = jnp.bfloat16, jnp.float32
YN, XN, ZN = 4, 4, 4
SECTS = 2 * YN
QB, CB, AN, DN = 112, 8, 128, 256
QN = QB * SECTS
BN = 16
GROUPS, ROWS = 2, 32
BLOCK = 4
CHUNKS = ((0, 0, 4), (0, 4, 4), (1, 0, 2), (1, 2, 2), (1, 4, 2), (1, 6, 2))
Z_LEADS = (0, 1, 0, 0, 0, 0)
STAGES = 14
STEP = QN // STAGES
Z_FIRST = (1, 1, 0, 1, 0, 0, 0, 1, 1, 0, 0, 1, 1, 1, 0, 0)
FAR_PLUS = (1, 1, 0, 0, 1, 1, 0, 0, 1, 1, 0, 0, 1, 1, 0, 1)


def kernel(counts, left, lam, right, out,
           lbuf, ltra, ltrb, ltr, mbuf, rstage, rmat, coul, p32, pbf, rpair,
           s32, sbf, xdir, u32, ubf, zdir,
           v32, acc, acc0, lown, mown, in_sem, rsem, ag_send, ag_recv, hello, pr_send, pr_recv, x_send, x_recv, z_send, z_recv):
    sect, tile = lax.axis_index("sect"), lax.axis_index("tile")
    zl, y = sect // YN, sect % YN
    zh, x, core = tile // (2 * XN), (tile // 2) % XN, tile % 2
    base, obase = zl * YN, (1 - zl) * YN
    yp, ym, yf = (y + 1) % YN, (y + YN - 1) % YN, (y + 2) % YN
    at_yp, at_ym, at_z = {"sect": base + yp}, {"sect": base + ym}, {"sect": obase + y}

    bm, bp, bf = base + ym, base + yp, base + yf
    oy, om, op, of = obase + y, obase + ym, obase + yp, obase + yf

    def tile_at(zz, xx, cc):
        return {"tile": (zz * XN + xx) * 2 + cc}

    xp, xm, xf = (x + 1) % XN, (x + XN - 1) % XN, (x + 2) % XN
    zp, zm, zf = (zh + 1) % ZN, (zh + ZN - 1) % ZN, (zh + 2) % ZN
    at_xp, at_xm = tile_at(zh, xp, core), tile_at(zh, xm, core)
    at_zp, at_zm = tile_at(zp, x, core), tile_at(zm, x, core)
    at_xf, at_zf = tile_at(zh, xf, core), tile_at(zf, x, core)
    at_pair = tile_at(zh, x, 1 - core)

    barrier = pltpu.get_barrier_semaphore()
    friends = (at_yp, at_ym, at_z, at_xp, at_xm, at_zp, at_zm, at_pair)
    for friend in friends:
        pl.semaphore_signal(barrier, inc=1, device_id=friend, device_id_type=MESH)

    def stage_copy(k):
        rows = pl.ds(k * STEP, STEP)
        return pltpu.make_async_copy(right.at[rows], rstage.at[rows], rsem.at[k])

    pltpu.make_async_copy(left, lown, in_sem.at[0]).start()
    pltpu.make_async_copy(lam, mown, in_sem.at[1]).start()
    for k in range(STAGES):
        stage_copy(k).start()

    n1, n2 = counts[0], counts[1]
    left_copy = pltpu.make_async_copy(left, lown, in_sem.at[0])
    lam_copy = pltpu.make_async_copy(lam, mown, in_sem.at[1])
    left_copy.wait()
    own = pltpu.einshape("qca->cqa", lown[...])
    lane = lax.broadcasted_iota(jnp.int32, (QB, AN), 1)
    for c in range(CB):
        orbital = tile * CB + c
        room = jnp.where(orbital < AN, n1 - orbital, n2 + AN - orbital)
        limit = jnp.where(room > 0, n1, 0)
        kept = jnp.where(lane < limit, own[c].astype(F32), 0.0).astype(BF)
        lbuf[c, pl.ds(pl.multiple_of(sect * QB, 16), QB), :] = kept
    lane = lax.broadcasted_iota(jnp.int32, (ROWS, DN), 1)
    d_live = lane < jnp.where(lane < AN, n1, n2 + AN)
    lam_copy.wait()
    for g in range(GROUPS):
        mine = jnp.concatenate([mown[16 * u + 8 * g : 16 * u + 8 * g + 8] for u in range(4)], axis=0)
        mine = pltpu.einshape("icd->cid", mine)
        for c in range(CB):
            kept = jnp.where(d_live, mine[c].astype(F32), 0.0).astype(BF)
            mbuf[g, pl.ds(pl.multiple_of(sect * ROWS, 16), ROWS), c * DN : (c + 1) * DN] = kept

    sent = []

    def go(make):
        make().start()
        sent.append(make)

    def piece(p, src):
        if p < 8:
            return lbuf.at[p, pl.ds(pl.multiple_of(src * QB, 16), QB), :]
        g, part = divmod(p - 8, 4)
        return mbuf.at[g, pl.ds(pl.multiple_of(src * ROWS, 16), ROWS), pl.ds(part * 2 * DN, 2 * DN)]

    def pass_on(p, src, k, where):
        def make():
            ref = piece(p, src)
            return pltpu.make_async_remote_copy(ref, ref, ag_send.at[p, k], ag_recv.at[p, src], where, MESH)

        go(make)

    def arrived(p, src):
        ref = piece(p, src)
        pltpu.make_async_remote_copy(ref, ref, ag_send.at[p, 0], ag_recv.at[p, src], at_z, MESH).wait_recv()

    def ag_own(p):
        if Z_FIRST[p]:
            pass_on(p, sect, 0, at_z)
        pass_on(p, sect, 1, at_yp)
        pass_on(p, sect, 2, at_ym)
        if not Z_FIRST[p]:
            pass_on(p, sect, 0, at_z)

    def ag_near(p):
        if Z_FIRST[p]:
            arrived(p, oy)
            pass_on(p, oy, 4, at_yp)
            pass_on(p, oy, 5, at_ym)
        arrived(p, bm)
        if FAR_PLUS[p]:
            pass_on(p, bm, 3, at_yp)
        if not Z_FIRST[p]:
            pass_on(p, bm, 4, at_z)
        arrived(p, bp)
        if not FAR_PLUS[p]:
            pass_on(p, bp, 3, at_ym)
        if not Z_FIRST[p]:
            pass_on(p, bp, 5, at_z)

    def ag_far(p):
        if Z_FIRST[p]:
            arrived(p, om)
            if FAR_PLUS[p]:
                pass_on(p, om, 6, at_yp)
            arrived(p, op)
            if not FAR_PLUS[p]:
                pass_on(p, op, 6, at_ym)
        else:
            arrived(p, bf)
            pass_on(p, bf, 6, at_z)

    def ag_half(p):
        if Z_FIRST[p]:
            arrived(p, bf)

    def ag_end(p):
        if Z_FIRST[p]:
            if p >= 4:
                arrived(p, bf)
            arrived(p, of)
        else:
            for src in (oy, om, op, of):
                arrived(p, src)

    def run(*todo):
        for event in todo:
            event()

    def loop(count, body, events):
        def step(j, carry):
            body(j)
            for k, todo in events.items():
                pl.when(j == k)(functools.partial(run, *todo))
            return carry

        lax.fori_loop(0, count, step, 0)

    def relay(events):
        def body(k):
            stage_copy(k).wait()
            rows = pl.ds(pl.multiple_of(k * STEP, 16), STEP)
            rmat[:, rows, :] = pltpu.einshape("qbd->bqd", rstage[rows])

        loop(STAGES, body, events)

    def layer(which):
        return pl.ds(pl.multiple_of(which * (QN // 2), 16), QN // 2)

    def turn_a():
        for c in range(4):
            ltra[c * AN : (c + 1) * AN, :] = lbuf[c, layer(zl), :].T

    def turn_b():
        for c in range(4):
            ltrb[c * AN : (c + 1) * AN, :] = lbuf[c, layer(1 - zl), :].T

    def turn_1():
        for c in range(4):
            ltr[c * AN : (c + 1) * AN, :] = lbuf[4 + c].T

    def keep(b, first, block):
        for k in range(4):
            c = first + k
            coul[b, :, c * DN : (c + 1) * DN] = block[k * AN : (k + 1) * AN].astype(BF)

    def coulomb_a(events):
        def body(j):
            for k in range(BLOCK):
                b = BLOCK * j + k
                acc0[b] = jnp.dot(ltra[...], rmat[b, layer(zl), :], preferred_element_type=F32)

        loop(BN // BLOCK, body, events)

    def coulomb_b(events):
        def body(j):
            for k in range(BLOCK):
                b = BLOCK * j + k
                keep(b, 0, acc0[b] + jnp.dot(ltrb[...], rmat[b, layer(1 - zl), :], preferred_element_type=F32))

        loop(BN // BLOCK, body, events)

    def coulomb_1(events):
        def body(j):
            for k in range(BLOCK):
                b = BLOCK * j + k
                keep(b, 4, jnp.dot(ltr[...], rmat[b], preferred_element_type=F32))

        loop(BN // BLOCK, body, events)

    def product(g, quad, first, last):
        cols = coul[4 * quad : 4 * quad + 4, :, first * DN : last * DN].reshape(4 * AN, (last - first) * DN)
        rows = mbuf[g, :, first * DN : last * DN]
        return lax.dot_general(rows, cols, (((1,), (1,)), ((), ())), preferred_element_type=F32)

    def early():
        for quad in range(BN // 4):
            acc[quad] = product(1, quad, 0, CB // 2)

    def ladder(t):
        g, first, count = CHUNKS[t]
        for quad in range(first // 2, (first + count) // 2):
            block = product(g, quad, 0, CB) if g == 0 else acc[quad] + product(g, quad, CB // 2, CB)
            for m in range(2):
                part = block[:, 2 * AN * m : 2 * AN * (m + 1)].reshape(ZN, XN, 2, 8, 2 * AN)
                part = jnp.concatenate([part[..., :AN], part[..., AN:]], axis=3)
                for cc in range(2):
                    for xx in range(XN):
                        p32[g, cc, xx, :, 2 * quad + m] = part[:, xx, cc]
                        pbf[g, cc, xx, :, 2 * quad + m] = part[:, xx, cc].astype(BF)

    def part_of(t):
        g, first, count = CHUNKS[t]
        return g, pl.ds(first, count)

    def pair_copy(t):
        g, js = part_of(t)
        return pltpu.make_async_remote_copy(
            pbf.at[g, 1 - core, :, :, js], rpair.at[g, :, :, js], pr_send.at[t], pr_recv.at[t], at_pair, MESH)

    x_ends, z_ends = ((xf, at_xf), (xp, at_xp), (xm, at_xm)), ((zf, at_zf), (zp, at_zp), (zm, at_zm))

    def first_copies(t, k):
        g, js = part_of(t)
        to, where = (z_ends if Z_LEADS[t] else x_ends)[k]
        src = sbf.at[g, :, to, js] if Z_LEADS[t] else sbf.at[g, to, :, js]
        return pltpu.make_async_remote_copy(src, xdir.at[g, k, :, js], x_send.at[t, k], x_recv.at[t, k], where, MESH)

    def last_copies(t, k):
        g, js = part_of(t)
        to, where = (x_ends if Z_LEADS[t] else z_ends)[k]
        return pltpu.make_async_remote_copy(
            ubf.at[g, to, js], zdir.at[g, k, js], z_send.at[t, k], z_recv.at[t, k], where, MESH)

    def red1(t):
        go(functools.partial(pair_copy, t))

    def red2(t):
        g, js = part_of(t)
        pair_copy(t).wait_recv()
        for xx in range(XN):
            total = p32[g, core, xx, :, js] + rpair[g, xx, :, js].astype(F32)
            s32[g, xx, :, js] = total
            sbf[g, xx, :, js] = total.astype(BF)
        for k in range(3):
            go(functools.partial(first_copies, t, k))

    def red4(t):
        g, js = part_of(t)
        for k in range(3):
            first_copies(t, k).wait_recv()
        total = s32[g, :, zh, js] if Z_LEADS[t] else s32[g, x, :, js]
        for k in range(3):
            total = total + xdir[g, k, :, js].astype(F32)
        u32[g, :, js] = total
        ubf[g, :, js] = total.astype(BF)
        for k in range(3):
            go(functools.partial(last_copies, t, k))

    def red6(t):
        g, js = part_of(t)
        for k in range(3):
            last_copies(t, k).wait_recv()
        total = u32[g, x if Z_LEADS[t] else zh, js]
        for k in range(3):
            total = total + zdir[g, k, js].astype(F32)
        v32[g, js] = total

    def greet():
        pl.semaphore_wait(hello, 4)

    def finish(g):
        summed = pltpu.einshape("bia->iba", v32[g].reshape(BN, 8, AN))
        orbital = sect * BN + lax.broadcasted_iota(jnp.int32, summed.shape, 1)
        out[8 * g : 8 * g + 8] = jnp.where(orbital < n2, summed, 0.0).astype(BF)

    o, n, f, e, h = ([functools.partial(act, p) for p in range(16)] for act in (ag_own, ag_near, ag_far, ag_end, ag_half))
    done = functools.partial(finish, 0)
    r1, r2, r4, r6 = ([functools.partial(act, t) for t in range(len(CHUNKS))] for act in (red1, red2, red4, red6))

    pl.semaphore_wait(barrier, len(friends))
    for friend in (at_xp, at_xm, at_zp, at_zm):
        pl.semaphore_signal(hello, inc=1, device_id=friend, device_id_type=MESH)

    run(o[0], o[1], o[2], o[3], o[4], o[5], o[6], o[7])
    relay({9: (n[0],), 11: (n[1],)})
    run(n[2], n[3], n[4], n[5], n[6], n[7], f[0], o[8], f[1], f[2], o[9], h[0], h[1], h[2], h[3])
    turn_a()
    run(o[10], f[3])
    coulomb_a({0: (f[4], f[6],), 1: (o[11], f[5], f[7],), 2: (o[12],)})
    run(o[13], n[8], e[0], e[1], e[2], e[3])
    turn_b()
    run(n[9], o[14])
    coulomb_b({0: (n[10],), 1: (o[15], n[11],)})
    run(n[12], f[8], e[4], e[5], e[6], e[7])
    turn_1()
    run(n[13])
    coulomb_1({0: (f[9], f[10], n[14],), 1: (n[15], f[11],), 2: (f[12],)})
    run(f[14], f[13], e[8], e[9], e[10], e[11])
    ladder(0)
    run(r1[0], f[15])
    ladder(1)
    run(r1[1], e[12], e[13])
    early()
    run(greet, r2[0], r2[1], e[14], e[15])
    ladder(2)
    run(r1[2])
    ladder(3)
    run(r1[3])
    ladder(4)
    run(r1[4])
    ladder(5)
    run(r1[5], r2[2], r2[3], r2[4], r2[5], r4[0], r4[2], r4[3], r4[1], r4[4], r4[5], r6[0], r6[2], r6[1], done, r6[3], r6[4], r6[5])
    finish(1)
    for make in sent:
        make().wait_send()


def per_device(irrep_counts, chol_left, chol_right, lam):
    spot = (BN // 2, 16, AN)
    vmem = pltpu.VMEM
    dma = pltpu.SemaphoreType.DMA
    summed = pl.pallas_call(
        kernel,
        out_shape=jax.ShapeDtypeStruct((GROUPS * 8, BN, AN), BF),
        in_specs=[
            pl.BlockSpec(memory_space=pltpu.SMEM),
            pl.BlockSpec(memory_space=pl.ANY),
            pl.BlockSpec(memory_space=pl.ANY),
            pl.BlockSpec(memory_space=pl.ANY),
        ],
        out_specs=pl.BlockSpec(memory_space=vmem),
        scratch_shapes=[
            vmem((CB, QN, AN), BF),
            vmem((4 * AN, QN // 2), BF),
            vmem((4 * AN, QN // 2), BF),
            vmem((4 * AN, QN), BF),
            vmem((GROUPS, ROWS * SECTS, CB * DN), BF),
            vmem((QN, BN, DN), BF),
            vmem((BN, QN, DN), BF),
            vmem((BN, AN, CB * DN), BF),
            vmem((GROUPS, 2, XN, ZN) + spot, F32),
            vmem((GROUPS, 2, XN, ZN) + spot, BF),
            vmem((GROUPS, XN, ZN) + spot, BF),
            vmem((GROUPS, XN, ZN) + spot, F32),
            vmem((GROUPS, XN, ZN) + spot, BF),
            vmem((GROUPS, 3, ZN) + spot, BF),
            vmem((GROUPS, ZN) + spot, F32),
            vmem((GROUPS, ZN) + spot, BF),
            vmem((GROUPS, 3) + spot, BF),
            vmem((GROUPS,) + spot, F32),
            vmem((BN // 4, ROWS * SECTS, 4 * AN), F32),
            vmem((BN, 4 * AN, DN), F32),
            vmem((QB, CB, AN), BF),
            vmem((SECTS * 8, CB, DN), BF),
            dma((2,)),
            dma((STAGES,)),
            dma((16, 7)),
            dma((16, SECTS)),
            pltpu.SemaphoreType.REGULAR,
            dma((len(CHUNKS),)),
            dma((len(CHUNKS),)),
            dma((len(CHUNKS), 3)),
            dma((len(CHUNKS), 3)),
            dma((len(CHUNKS), 3)),
            dma((len(CHUNKS), 3)),
        ],
        compiler_params=pltpu.CompilerParams(
            collective_id=0, has_side_effects=True, vmem_limit_bytes=56 << 20
        ),
        cost_estimate=pl.CostEstimate(flops=12_000_000_000, bytes_accessed=8_000_000, transcendentals=0),
    )(irrep_counts, chol_left, lam, chol_right)
    return jnp.transpose(summed, (0, 2, 1))


def solution(mesh):
    return jax.shard_map(
        per_device,
        mesh=mesh,
        in_specs=(P(), P("sect", "tile", None), P(None, "sect", None), P("sect", "tile", None)),
        out_specs=P("tile", None, "sect"),
        check_vma=False,
    )
```

```python
import functools

import jax
import jax.numpy as jnp
from jax import lax
from jax.experimental import pallas as pl
from jax.experimental.pallas import tpu as pltpu
from jax.sharding import PartitionSpec as P

MESH = pl.DeviceIdType.MESH
BF, F32 = jnp.bfloat16, jnp.float32
YN, XN, ZN = 4, 4, 4
SECTS = 2 * YN
QB, CB, AN, DN = 112, 8, 128, 256
QN = QB * SECTS
BN = 16
GROUPS, ROWS = 2, 32
BLOCK = 4
CHUNKS = ((0, 0, 4), (0, 4, 4), (1, 0, 2), (1, 2, 2), (1, 4, 2), (1, 6, 2))
Z_LEADS = (0, 0, 0, 1, 0, 0)
STAGES = 14
STEP = QN // STAGES
Z_FIRST = (1, 1, 0, 1, 0, 0, 1, 0, 1, 0, 1, 0, 1, 1, 1, 0)
FAR_PLUS = (1, 1, 0, 0, 1, 1, 0, 0, 1, 0, 0, 1, 1, 1, 1, 1)


def kernel(counts, left, lam, right, out,
           lbuf, ltra, ltrb, ltr, mbuf, rstage, rmat, coul, p32, pbf, rpair,
           s32, sbf, xdir, u32, ubf, zdir,
           v32, acc, acc0, lown, mown, in_sem, rsem, ag_send, ag_recv, hello, pr_send, pr_recv, x_send, x_recv, z_send, z_recv):
    sect, tile = lax.axis_index("sect"), lax.axis_index("tile")
    zl, y = sect // YN, sect % YN
    zh, x, core = tile // (2 * XN), (tile // 2) % XN, tile % 2
    base, obase = zl * YN, (1 - zl) * YN
    yp, ym, yf = (y + 1) % YN, (y + YN - 1) % YN, (y + 2) % YN
    at_yp, at_ym, at_z = {"sect": base + yp}, {"sect": base + ym}, {"sect": obase + y}

    bm, bp, bf = base + ym, base + yp, base + yf
    oy, om, op, of = obase + y, obase + ym, obase + yp, obase + yf

    def tile_at(zz, xx, cc):
        return {"tile": (zz * XN + xx) * 2 + cc}

    xp, xm, xf = (x + 1) % XN, (x + XN - 1) % XN, (x + 2) % XN
    zp, zm, zf = (zh + 1) % ZN, (zh + ZN - 1) % ZN, (zh + 2) % ZN
    at_xp, at_xm = tile_at(zh, xp, core), tile_at(zh, xm, core)
    at_zp, at_zm = tile_at(zp, x, core), tile_at(zm, x, core)
    at_xf, at_zf = tile_at(zh, xf, core), tile_at(zf, x, core)
    at_pair = tile_at(zh, x, 1 - core)

    barrier = pltpu.get_barrier_semaphore()
    friends = (at_yp, at_ym, at_z, at_xp, at_xm, at_zp, at_zm, at_pair)
    for friend in friends:
        pl.semaphore_signal(barrier, inc=1, device_id=friend, device_id_type=MESH)

    def stage_copy(k):
        rows = pl.ds(k * STEP, STEP)
        return pltpu.make_async_copy(right.at[rows], rstage.at[rows], rsem.at[k])

    pltpu.make_async_copy(left, lown, in_sem.at[0]).start()
    pltpu.make_async_copy(lam, mown, in_sem.at[1]).start()
    for k in range(STAGES):
        stage_copy(k).start()

    n1, n2 = counts[0], counts[1]
    left_copy = pltpu.make_async_copy(left, lown, in_sem.at[0])
    lam_copy = pltpu.make_async_copy(lam, mown, in_sem.at[1])
    left_copy.wait()
    own = pltpu.einshape("qca->cqa", lown[...])
    lane = lax.broadcasted_iota(jnp.int32, (QB, AN), 1)
    for c in range(CB):
        orbital = tile * CB + c
        room = jnp.where(orbital < AN, n1 - orbital, n2 + AN - orbital)
        limit = jnp.where(room > 0, n1, 0)
        kept = jnp.where(lane < limit, own[c].astype(F32), 0.0).astype(BF)
        lbuf[c, pl.ds(pl.multiple_of(sect * QB, 16), QB), :] = kept
    lane = lax.broadcasted_iota(jnp.int32, (ROWS, DN), 1)
    d_live = lane < jnp.where(lane < AN, n1, n2 + AN)
    lam_copy.wait()
    for g in range(GROUPS):
        mine = jnp.concatenate([mown[16 * u + 8 * g : 16 * u + 8 * g + 8] for u in range(4)], axis=0)
        mine = pltpu.einshape("icd->cid", mine)
        for c in range(CB):
            kept = jnp.where(d_live, mine[c].astype(F32), 0.0).astype(BF)
            mbuf[g, pl.ds(pl.multiple_of(sect * ROWS, 16), ROWS), c * DN : (c + 1) * DN] = kept

    sent = []

    def go(make):
        make().start()
        sent.append(make)

    def piece(p, src):
        if p < 8:
            return lbuf.at[p, pl.ds(pl.multiple_of(src * QB, 16), QB), :]
        g, part = divmod(p - 8, 4)
        return mbuf.at[g, pl.ds(pl.multiple_of(src * ROWS, 16), ROWS), pl.ds(part * 2 * DN, 2 * DN)]

    def pass_on(p, src, k, where):
        def make():
            ref = piece(p, src)
            return pltpu.make_async_remote_copy(ref, ref, ag_send.at[p, k], ag_recv.at[p, src], where, MESH)

        go(make)

    def arrived(p, src):
        ref = piece(p, src)
        pltpu.make_async_remote_copy(ref, ref, ag_send.at[p, 0], ag_recv.at[p, src], at_z, MESH).wait_recv()

    def ag_own(p):
        if Z_FIRST[p]:
            pass_on(p, sect, 0, at_z)
        pass_on(p, sect, 1, at_yp)
        pass_on(p, sect, 2, at_ym)
        if not Z_FIRST[p]:
            pass_on(p, sect, 0, at_z)

    def ag_near(p):
        if Z_FIRST[p]:
            arrived(p, oy)
            pass_on(p, oy, 4, at_yp)
            pass_on(p, oy, 5, at_ym)
        arrived(p, bm)
        if FAR_PLUS[p]:
            pass_on(p, bm, 3, at_yp)
        if not Z_FIRST[p]:
            pass_on(p, bm, 4, at_z)
        arrived(p, bp)
        if not FAR_PLUS[p]:
            pass_on(p, bp, 3, at_ym)
        if not Z_FIRST[p]:
            pass_on(p, bp, 5, at_z)

    def ag_far(p):
        if Z_FIRST[p]:
            arrived(p, om)
            if FAR_PLUS[p]:
                pass_on(p, om, 6, at_yp)
            arrived(p, op)
            if not FAR_PLUS[p]:
                pass_on(p, op, 6, at_ym)
        else:
            arrived(p, bf)
            pass_on(p, bf, 6, at_z)

    def ag_half(p):
        if Z_FIRST[p]:
            arrived(p, bf)

    def ag_end(p):
        if Z_FIRST[p]:
            if p >= 4:
                arrived(p, bf)
            arrived(p, of)
        else:
            for src in (oy, om, op, of):
                arrived(p, src)

    def run(*todo):
        for event in todo:
            event()

    def loop(count, body, events):
        def step(j, carry):
            body(j)
            for k, todo in events.items():
                pl.when(j == k)(functools.partial(run, *todo))
            return carry

        lax.fori_loop(0, count, step, 0)

    def relay(events):
        def body(k):
            stage_copy(k).wait()
            rows = pl.ds(pl.multiple_of(k * STEP, 16), STEP)
            rmat[:, rows, :] = pltpu.einshape("qbd->bqd", rstage[rows])

        loop(STAGES, body, events)

    def layer(which):
        return pl.ds(pl.multiple_of(which * (QN // 2), 16), QN // 2)

    def turn_a():
        for c in range(4):
            ltra[c * AN : (c + 1) * AN, :] = lbuf[c, layer(zl), :].T

    def turn_b():
        for c in range(4):
            ltrb[c * AN : (c + 1) * AN, :] = lbuf[c, layer(1 - zl), :].T

    def turn_1():
        for c in range(4):
            ltr[c * AN : (c + 1) * AN, :] = lbuf[4 + c].T

    def keep(b, first, block):
        for k in range(4):
            c = first + k
            coul[b, :, c * DN : (c + 1) * DN] = block[k * AN : (k + 1) * AN].astype(BF)

    def coulomb_a(events):
        def body(j):
            for k in range(BLOCK):
                b = BLOCK * j + k
                acc0[b] = jnp.dot(ltra[...], rmat[b, layer(zl), :], preferred_element_type=F32)

        loop(BN // BLOCK, body, events)

    def coulomb_b(events):
        def body(j):
            for k in range(BLOCK):
                b = BLOCK * j + k
                keep(b, 0, acc0[b] + jnp.dot(ltrb[...], rmat[b, layer(1 - zl), :], preferred_element_type=F32))

        loop(BN // BLOCK, body, events)

    def coulomb_1(events):
        def body(j):
            for k in range(BLOCK):
                b = BLOCK * j + k
                keep(b, 4, jnp.dot(ltr[...], rmat[b], preferred_element_type=F32))

        loop(BN // BLOCK, body, events)

    def product(g, quad, first, last):
        cols = coul[4 * quad : 4 * quad + 4, :, first * DN : last * DN].reshape(4 * AN, (last - first) * DN)
        rows = mbuf[g, :, first * DN : last * DN]
        return lax.dot_general(rows, cols, (((1,), (1,)), ((), ())), preferred_element_type=F32)

    def early():
        for quad in range(BN // 4):
            acc[quad] = product(1, quad, 0, CB // 2)

    def ladder(t):
        g, first, count = CHUNKS[t]
        for quad in range(first // 2, (first + count) // 2):
            block = product(g, quad, 0, CB) if g == 0 else acc[quad] + product(g, quad, CB // 2, CB)
            for m in range(2):
                part = block[:, 2 * AN * m : 2 * AN * (m + 1)].reshape(ZN, XN, 2, 8, 2 * AN)
                part = jnp.concatenate([part[..., :AN], part[..., AN:]], axis=3)
                for cc in range(2):
                    for xx in range(XN):
                        p32[g, cc, xx, :, 2 * quad + m] = part[:, xx, cc]
                        pbf[g, cc, xx, :, 2 * quad + m] = part[:, xx, cc].astype(BF)

    def part_of(t):
        g, first, count = CHUNKS[t]
        return g, pl.ds(first, count)

    def pair_copy(t):
        g, js = part_of(t)
        return pltpu.make_async_remote_copy(
            pbf.at[g, 1 - core, :, :, js], rpair.at[g, :, :, js], pr_send.at[t], pr_recv.at[t], at_pair, MESH)

    x_ends, z_ends = ((xf, at_xf), (xp, at_xp), (xm, at_xm)), ((zf, at_zf), (zp, at_zp), (zm, at_zm))

    def first_copies(t, k):
        g, js = part_of(t)
        to, where = (z_ends if Z_LEADS[t] else x_ends)[k]
        src = sbf.at[g, :, to, js] if Z_LEADS[t] else sbf.at[g, to, :, js]
        return pltpu.make_async_remote_copy(src, xdir.at[g, k, :, js], x_send.at[t, k], x_recv.at[t, k], where, MESH)

    def last_copies(t, k):
        g, js = part_of(t)
        to, where = (x_ends if Z_LEADS[t] else z_ends)[k]
        return pltpu.make_async_remote_copy(
            ubf.at[g, to, js], zdir.at[g, k, js], z_send.at[t, k], z_recv.at[t, k], where, MESH)

    def red1(t):
        go(functools.partial(pair_copy, t))

    def red2(t):
        g, js = part_of(t)
        pair_copy(t).wait_recv()
        for xx in range(XN):
            total = p32[g, core, xx, :, js] + rpair[g, xx, :, js].astype(F32)
            s32[g, xx, :, js] = total
            sbf[g, xx, :, js] = total.astype(BF)
        for k in range(3):
            go(functools.partial(first_copies, t, k))

    def red4(t):
        g, js = part_of(t)
        for k in range(3):
            first_copies(t, k).wait_recv()
        total = s32[g, :, zh, js] if Z_LEADS[t] else s32[g, x, :, js]
        for k in range(3):
            total = total + xdir[g, k, :, js].astype(F32)
        u32[g, :, js] = total
        ubf[g, :, js] = total.astype(BF)
        for k in range(3):
            go(functools.partial(last_copies, t, k))

    def red6(t):
        g, js = part_of(t)
        for k in range(3):
            last_copies(t, k).wait_recv()
        total = u32[g, x if Z_LEADS[t] else zh, js]
        for k in range(3):
            total = total + zdir[g, k, js].astype(F32)
        v32[g, js] = total

    def greet():
        pl.semaphore_wait(hello, 4)

    def finish(g):
        summed = pltpu.einshape("bia->iba", v32[g].reshape(BN, 8, AN))
        orbital = sect * BN + lax.broadcasted_iota(jnp.int32, summed.shape, 1)
        out[8 * g : 8 * g + 8] = jnp.where(orbital < n2, summed, 0.0).astype(BF)

    o, n, f, e, h = ([functools.partial(act, p) for p in range(16)] for act in (ag_own, ag_near, ag_far, ag_end, ag_half))
    done = functools.partial(finish, 0)
    r1, r2, r4, r6 = ([functools.partial(act, t) for t in range(len(CHUNKS))] for act in (red1, red2, red4, red6))

    pl.semaphore_wait(barrier, len(friends))
    for friend in (at_xp, at_xm, at_zp, at_zm):
        pl.semaphore_signal(hello, inc=1, device_id=friend, device_id_type=MESH)

    run(o[0], o[1], o[2], o[3])
    relay({2: (o[4],), 4: (o[5],), 6: (o[6],), 8: (o[7], n[0],), 10: (n[1],), 12: (n[2],)})
    run(n[3], n[4], n[5], o[8], n[6], n[7], f[0], o[9], f[1], f[2], o[10], h[0], h[1], h[2], h[3])
    turn_a()
    run(f[3])
    coulomb_a({0: (f[4], o[11],), 1: (f[5], n[8],), 2: (f[6], f[7], o[12],)})
    run(n[9], o[13], e[0], e[1], e[2], e[3])
    turn_b()
    coulomb_b({0: (n[10],), 1: (n[11], o[14],), 2: (f[8], o[15],)})
    run(n[12], f[9], e[4], e[5], e[6], e[7])
    turn_1()
    coulomb_1({0: (f[10], n[13],), 1: (f[11],), 2: (n[14], n[15],)})
    run(f[12], e[8], e[9], e[10], e[11])
    ladder(0)
    run(r1[0], f[13])
    ladder(1)
    run(r1[1], f[14], greet, r2[0], f[15], e[12], e[13])
    early()
    run(r2[1], e[14], e[15])
    ladder(2)
    run(r1[2])
    ladder(3)
    run(r1[3])
    ladder(4)
    run(r1[4], r4[0], r2[2])
    ladder(5)
    run(r1[5], r2[3], r2[4], r4[1], r2[5], r4[2], r6[0], r4[4], r4[5], r4[3], r6[1], done, r6[2], r6[3], r6[4], r6[5])
    finish(1)
    for make in sent:
        make().wait_send()


def per_device(irrep_counts, chol_left, chol_right, lam):
    spot = (BN // 2, 16, AN)
    vmem = pltpu.VMEM
    dma = pltpu.SemaphoreType.DMA
    summed = pl.pallas_call(
        kernel,
        out_shape=jax.ShapeDtypeStruct((GROUPS * 8, BN, AN), BF),
        in_specs=[
            pl.BlockSpec(memory_space=pltpu.SMEM),
            pl.BlockSpec(memory_space=pl.ANY),
            pl.BlockSpec(memory_space=pl.ANY),
            pl.BlockSpec(memory_space=pl.ANY),
        ],
        out_specs=pl.BlockSpec(memory_space=vmem),
        scratch_shapes=[
            vmem((CB, QN, AN), BF),
            vmem((4 * AN, QN // 2), BF),
            vmem((4 * AN, QN // 2), BF),
            vmem((4 * AN, QN), BF),
            vmem((GROUPS, ROWS * SECTS, CB * DN), BF),
            vmem((QN, BN, DN), BF),
            vmem((BN, QN, DN), BF),
            vmem((BN, AN, CB * DN), BF),
            vmem((GROUPS, 2, XN, ZN) + spot, F32),
            vmem((GROUPS, 2, XN, ZN) + spot, BF),
            vmem((GROUPS, XN, ZN) + spot, BF),
            vmem((GROUPS, XN, ZN) + spot, F32),
            vmem((GROUPS, XN, ZN) + spot, BF),
            vmem((GROUPS, 3, ZN) + spot, BF),
            vmem((GROUPS, ZN) + spot, F32),
            vmem((GROUPS, ZN) + spot, BF),
            vmem((GROUPS, 3) + spot, BF),
            vmem((GROUPS,) + spot, F32),
            vmem((BN // 4, ROWS * SECTS, 4 * AN), F32),
            vmem((BN, 4 * AN, DN), F32),
            vmem((QB, CB, AN), BF),
            vmem((SECTS * 8, CB, DN), BF),
            dma((2,)),
            dma((STAGES,)),
            dma((16, 7)),
            dma((16, SECTS)),
            pltpu.SemaphoreType.REGULAR,
            dma((len(CHUNKS),)),
            dma((len(CHUNKS),)),
            dma((len(CHUNKS), 3)),
            dma((len(CHUNKS), 3)),
            dma((len(CHUNKS), 3)),
            dma((len(CHUNKS), 3)),
        ],
        compiler_params=pltpu.CompilerParams(
            collective_id=0, has_side_effects=True, vmem_limit_bytes=56 << 20
        ),
        cost_estimate=pl.CostEstimate(flops=12_000_000_000, bytes_accessed=8_000_000, transcendentals=0),
    )(irrep_counts, chol_left, lam, chol_right)
    return jnp.transpose(summed, (0, 2, 1))


def solution(mesh):
    return jax.shard_map(
        per_device,
        mesh=mesh,
        in_specs=(P(), P("sect", "tile", None), P(None, "sect", None), P("sect", "tile", None)),
        out_specs=P("tile", None, "sect"),
        check_vma=False,
    )
```
